512 devices in a mesh: query: 2 (over core), key: 8 (over x, y_hi), heads: 32 (over z, y_lo).
Axes of the slice: x: 4, y: 4 (y_hi: 2, y_lo: 2; y = y_hi * 2 + y_lo), z: 16, core: 2. Of those that a mesh axis runs over, the one named last changes fastest.
Arguments:
- pair_feats: bfloat16 [1024, 64, 8192], P(('query', 'heads'), None, 'key'), may hold values from -6 to 6
- bucket_ids: int32 [1024, 8192], P(('query', 'heads'), 'key'), may hold values from 0 to 31
- ln_gain: float32 [64], replicated, may hold values from 0.5 to 1.5
- w_in: bfloat16 [64, 256], replicated, may hold values from -0.75 to 0.75
- b_in: float32 [256], replicated, may hold values from -3 to 3
- w_out: bfloat16 [256, 32], replicated, may hold values from -0.375 to 0.375
- bucket_table: bfloat16 [32, 32], replicated, may hold values from -4 to 4
- key_mask: int32 [8192], P('key'), may hold values 0 or 1
- q_heads: bfloat16 [32, 32, 1024], P('heads', None, 'query'), may hold values from -6 to 6
- k_heads: bfloat16 [32, 32, 8192], P('heads', None, 'key'), may hold values from -6 to 6
- v_heads: bfloat16 [32, 32, 8192], P('heads', None, 'key'), may hold values from -6 to 6
- out_heads: bfloat16 [32, 32, 1024], P('heads', None, 'query'), may hold values from -6 to 6
- dout_heads: bfloat16 [32, 32, 1024], P('heads', None, 'query'), may hold values from -96 to 96
- log_norm: float32 [32, 1024], P('heads', 'query'), may hold values from 8 to 10
Outputs:
- grad_pairs: bfloat16 [1024, 64, 8192], P(('query', 'heads'), None, 'key')
- grad_q: bfloat16 [32, 32, 1024], P('heads', None, 'query')
- grad_k: bfloat16 [32, 32, 8192], P('heads', None, 'key')
- grad_v: bfloat16 [32, 32, 8192], P('heads', None, 'key')
The draws below stay inside these ranges and needn't reach their ends.
All inputs are finite; a program needn't handle non-finite values. No bound on the sum of `key_mask` on one device may be relied on, other than what follows from the above.
Results may differ from the reference program's by a relative error of at most 0.012.
The reference program's roundings to bfloat16 on the way (of `normed`, `hidden`, `bias_vals`, `probs_low`, `dscores` and `dpre`) count: a program that leaves them out, or rounds other values in their place, can miss the bound.
Values may be sent and summed in bfloat16 or wider, within the bound.
A program may use at most 64 MiB of HBM per device.

```python
import math
import jax
import jax.numpy as jnp
from jax import lax

C = 64
HID = 256
H = 32
DH = 32
BUCKETS = 32
NQ = 1024
NK = 8192


def place_ends(result, own_key, smallest, high):
    place = [jax.random.randint(jax.random.fold_in(own_key, axis), (), 0, length) for axis, length in enumerate(result.shape)]
    widest = result.shape.index(max(result.shape))
    next_to = place[:widest] + [(place[widest] + 1) % result.shape[widest]] + place[widest + 1:]
    return result.at[tuple(place)].set(smallest).at[tuple(next_to)].set(high)


def level_of(rng, extent, split, low, largest):
    def one(axis_at, parts):
        steps = jax.random.uniform(jax.random.fold_in(jax.random.fold_in(rng, 6), axis_at), (parts,), jnp.float32, low / len(split), largest / len(split))
        return jnp.repeat(jnp.exp(steps), extent[axis_at] // parts).reshape((-1,) + (1,) * (len(extent) - axis_at - 1))

    level = one(*split[0])
    for cut in split[1:]:
        level = level * one(*cut)
    return level


def normal_values(own_key, extent, scale, reach, cuts=(), held_as=jnp.bfloat16):
    loudness = level_of(own_key, extent, cuts, -0.22, 0.18) if cuts else 1.0
    result = jax.random.normal(own_key, extent, jnp.float32) * scale * loudness
    return jnp.minimum(jnp.maximum(result, -reach), reach).astype(held_as)


def setup_inputs(seed: int = 0) -> dict:
    keys = jax.random.split(jax.random.key(seed), 15)
    pair_feats = normal_values(keys[0], (NQ, C, NK), 1.0, 6.0, ((0, 64), (2, 8)))
    bucket_ids = place_ends(jax.random.randint(keys[1], (NQ, NK), 0, BUCKETS), jax.random.fold_in(keys[1], 1), 0, BUCKETS - 1).astype(jnp.int32)
    ln_gain = jnp.clip(1.0 + 0.1 * jax.random.normal(keys[2], (C,), jnp.float32), 0.5, 1.5)
    w_in = normal_values(keys[3], (C, HID), C ** -0.5, 0.75)
    b_in = normal_values(keys[4], (HID,), 0.5, 3.0, (), jnp.float32)
    w_out = normal_values(keys[5], (HID, H), HID ** -0.5, 0.375)
    bucket_table = normal_values(keys[6], (BUCKETS, H), 1.0, 4.0)
    key_mask = place_ends((jax.random.randint(keys[7], (NK,), 0, 8) < 7).astype(jnp.int32), jax.random.fold_in(keys[7], 1), 0, 1)
    q_heads = normal_values(keys[8], (H, DH, NQ), 1.0, 6.0, ((0, 32), (2, 2)))
    k_heads = normal_values(keys[9], (H, DH, NK), 1.0, 6.0, ((0, 32), (2, 8)))
    v_heads = normal_values(keys[10], (H, DH, NK), 1.0, 6.0, ((0, 32), (2, 8)))
    out_heads = normal_values(keys[11], (H, DH, NQ), 1.0, 6.0, ((0, 32), (2, 2)))
    dout_heads = normal_values(keys[12], (H, DH, NQ), 16.0, 96.0, ((0, 32), (2, 2)))
    log_norm = jnp.clip(8.0 + 2.0 * jax.random.uniform(keys[13], (H, NQ), jnp.float32) ** level_of(keys[13], (H, NQ), ((0, 32), (1, 2)), -0.2, 0.2), 8.0, 10.0)
    return {"pair_feats": pair_feats, "bucket_ids": bucket_ids, "ln_gain": ln_gain, "w_in": w_in, "b_in": b_in, "w_out": w_out, "bucket_table": bucket_table, "key_mask": key_mask, "q_heads": q_heads, "k_heads": k_heads, "v_heads": v_heads, "out_heads": out_heads, "dout_heads": dout_heads, "log_norm": log_norm}


def gelu_parts(pre_act):
    cdf_val = 0.5 * (1.0 + jax.scipy.special.erf(pre_act * (1.0 / math.sqrt(2.0))))
    density = jnp.exp(-0.5 * pre_act * pre_act) * (1.0 / math.sqrt(2.0 * math.pi))
    return (pre_act * cdf_val, cdf_val + pre_act * density)

def normalize(pair_blk, ln_gain):
    values = pair_blk.astype(jnp.float32)
    centre = values - lax.optimization_barrier(jnp.mean(values, axis=1, keepdims=True))
    inv_std = lax.rsqrt(lax.optimization_barrier(jnp.mean(centre * centre, axis=1, keepdims=True)) + 1e-05)
    unit_pairs = centre * inv_std
    normed = (unit_pairs * ln_gain[None, :, None]).astype(jnp.bfloat16)
    return (unit_pairs, inv_std, normed)

def make_bias(pair_blk, bucket_blk, ln_gain, w_in, b_in, w_out, bucket_table):
    unit_pairs, inv_std, normed = normalize(pair_blk, ln_gain)
    pre_act = jnp.einsum('rck,cf->rfk', normed.astype(jnp.float32), w_in.astype(jnp.float32)) + b_in[None, :, None]
    gelu_val, gelu_slope = gelu_parts(pre_act)
    hidden = gelu_val.astype(jnp.bfloat16)
    lookup = jnp.transpose(bucket_table[bucket_blk].astype(jnp.float32), (0, 2, 1))
    mixed = jnp.einsum('rfk,fh->rhk', hidden.astype(jnp.float32), w_out.astype(jnp.float32))
    return (mixed + lookup).astype(jnp.bfloat16)

def pair_grad(pair_blk, ln_gain, w_in, b_in, w_out, dscores):
    unit_pairs, inv_std, normed = normalize(pair_blk, ln_gain)
    pre_act = jnp.einsum('rck,cf->rfk', normed.astype(jnp.float32), w_in.astype(jnp.float32)) + b_in[None, :, None]
    gelu_val, gelu_slope = gelu_parts(pre_act)
    dhidden = jnp.einsum('rhk,fh->rfk', dscores.astype(jnp.float32), w_out.astype(jnp.float32))
    dpre = (dhidden * gelu_slope).astype(jnp.bfloat16)
    dunit = jnp.einsum('rfk,cf->rck', dpre.astype(jnp.float32), w_in.astype(jnp.float32)) * ln_gain[None, :, None]
    first_mean = lax.optimization_barrier(jnp.mean(dunit, axis=1, keepdims=True))
    second_mean = lax.optimization_barrier(jnp.mean(dunit * unit_pairs, axis=1, keepdims=True))
    return (inv_std * (dunit - first_mean - unit_pairs * second_mean)).astype(jnp.bfloat16)

def reference(pair_feats, bucket_ids, ln_gain, w_in, b_in, w_out, bucket_table, key_mask, q_heads, k_heads, v_heads, out_heads, dout_heads, log_norm):
    rows_per = math.gcd(NQ, 16)
    score_scale = 1.0 / math.sqrt(DH)
    key_live = (key_mask == 1)[None, None, :]
    keys_f32 = k_heads.astype(jnp.float32)
    values_f32 = v_heads.astype(jnp.float32)

    def row_step(running, counter):
        dk_acc, dv_acc = running
        begin_row = (counter * rows_per).astype(jnp.int32)
        pair_blk = lax.dynamic_slice_in_dim(pair_feats, begin_row, rows_per, 0)
        bucket_blk = lax.dynamic_slice_in_dim(bucket_ids, begin_row, rows_per, 0)
        q_blk = lax.dynamic_slice_in_dim(q_heads, begin_row, rows_per, 2).astype(jnp.float32)
        out_blk = lax.dynamic_slice_in_dim(out_heads, begin_row, rows_per, 2).astype(jnp.float32)
        dout_blk = lax.dynamic_slice_in_dim(dout_heads, begin_row, rows_per, 2).astype(jnp.float32)
        norm_blk = lax.dynamic_slice_in_dim(log_norm, begin_row, rows_per, 1)
        bias_vals = make_bias(pair_blk, bucket_blk, ln_gain, w_in, b_in, w_out, bucket_table)
        scores = jnp.einsum('hdi,hdj->hij', q_blk, keys_f32) * score_scale + jnp.transpose(bias_vals.astype(jnp.float32), (1, 0, 2))
        attn_probs = jnp.where(key_live, jnp.exp(scores - norm_blk[:, :, None]), 0.0)
        probs_low = attn_probs.astype(jnp.bfloat16)
        deltas = lax.optimization_barrier(jnp.sum(dout_blk * out_blk, axis=1))
        dprobs = jnp.einsum('hdi,hdj->hij', dout_blk, values_f32)
        dscores = (attn_probs * (dprobs - deltas[:, :, None])).astype(jnp.bfloat16)
        dscore_f = dscores.astype(jnp.float32)
        dv_acc = dv_acc + jnp.einsum('hdi,hij->hdj', dout_blk, probs_low.astype(jnp.float32))
        dk_acc = dk_acc + jnp.einsum('hdi,hij->hdj', q_blk, dscore_f)
        dq_blk = (jnp.einsum('hdj,hij->hdi', keys_f32, dscore_f) * score_scale).astype(jnp.bfloat16)
        grad_blk = pair_grad(pair_blk, ln_gain, w_in, b_in, w_out, jnp.transpose(dscores, (1, 0, 2)))
        return ((dk_acc, dv_acc), (dq_blk, grad_blk))
    zero_grad = jnp.zeros((H, DH, NK), jnp.float32)
    block_ids = jnp.arange(NQ // rows_per, dtype=jnp.int32)
    (dk_acc, dv_acc), (dq_blocks, grad_blocks) = lax.scan(row_step, (zero_grad, zero_grad), block_ids)
    grad_q = jnp.transpose(dq_blocks, (1, 2, 0, 3)).reshape(H, DH, NQ)
    grad_pairs = grad_blocks.reshape(NQ, C, NK)
    grad_k = (dk_acc * score_scale).astype(jnp.bfloat16)
    grad_v = dv_acc.astype(jnp.bfloat16)
    return (grad_pairs, grad_q, grad_k, grad_v)
```

```python
import functools
import math

import jax
import jax.numpy as jnp
from jax import lax
from jax.experimental import pallas as pl
from jax.experimental.pallas import tpu as pltpu
from jax.sharding import PartitionSpec as P

F32 = jnp.float32
BF16 = jnp.bfloat16
MESH = pl.DeviceIdType.MESH


def dot(lhs, rhs):
    return jnp.dot(lhs, rhs, preferred_element_type=F32)


def iota(shape, axis):
    return lax.broadcasted_iota(jnp.int32, shape, axis)


def ones_where(cond):
    return jnp.where(cond, 1.0, 0.0).astype(BF16)


def column(row):
    size = row.shape[1]
    diag = iota((size, size), 0) == iota((size, size), 1)
    return jnp.sum(jnp.where(diag, jnp.broadcast_to(row, (size, size)), 0.0), axis=1, keepdims=True)


def pieces(value):
    first = value.astype(BF16).astype(F32)
    second = (value - first).astype(BF16).astype(F32)
    third = (value - first - second).astype(BF16).astype(F32)
    return first, second, third


def gelu_parts(pre_act):
    cdf_val = 0.5 * (1.0 + lax.erf(pre_act * (1.0 / math.sqrt(2.0))))
    density = jnp.exp(-0.5 * pre_act * pre_act) * (1.0 / math.sqrt(2.0 * math.pi))
    return pre_act * cdf_val, cdf_val + pre_act * density


def kernel(
    x_hbm, bucket_hbm, gain_hbm, win_hbm, bin_hbm, woutt_hbm, table_hbm, mask_hbm,
    q_hbm, k_hbm, v_hbm, out_hbm, dout_hbm, norm_hbm,
    gp_hbm, gq_hbm, gk_hbm, gv_hbm,
    x_v, bucket_v, gain_v, win_v, bin_v, woutt_v, table_v, mask_v,
    q_v, out_v, dout_v, norm_v,
    gp_v, gq_v, gkv_v,
    slope_v, stat_v, kv_v, bias_out, bias_in, ds_all, ds_in, probs_v,
    qstage, qrecv, qblk_v, doblk_v, norm_b, delta_b, dkv_v,
    rsp_send, rsp_recv, rsm_send, rsm_recv,
    dq_send, dq_recv, dq_peers, w1_v, w2_v, wmix_v, tab_v,
    in_sem, x_sem, kv_sem, gp_sem, o_sem,
    ag_send, ag_recv, q_send, q_recv, b_send, b_recv, d_send, d_recv,
    rp_send, rp_recv, rm_send, rm_recv, f_send, f_recv,
    p1_send, p1_recv, p2_send, p2_recv,
):
    core = lax.axis_index("query")
    key = lax.axis_index("key")
    col = lax.axis_index("heads")
    zpos = col // 2
    ypos = col % 2
    home = zpos // 8
    slot = zpos % 8
    mine = core * 2 + ypos
    is_home = home == core
    score_scale = 1.0 / math.sqrt(32.0)

    def device(core_at, z_at, y_at):
        return (core_at, key, z_at * 2 + y_at)

    right = device(core, (zpos + 1) % 16, ypos)
    left = device(core, (zpos + 15) % 16, ypos)

    def quad(step):
        core_at = (core + step // 2) % 2
        y_at = (ypos + step % 2) % 2
        return device(core_at, zpos, y_at), core_at * 2 + y_at

    barrier = pltpu.get_barrier_semaphore()

    def greet(where):
        pl.semaphore_signal(barrier, inc=1, device_id=where, device_id_type=MESH)

    greet(right)
    greet(left)
    for step in (1, 2, 3):
        greet(quad(step)[0])

    def greet_z(at, carry):
        @pl.when(jnp.logical_not(jnp.logical_and(is_home, at == zpos)))
        def _():
            greet(device(home, at, ypos))

        @pl.when(jnp.logical_not(jnp.logical_and(core == at // 8, core * 8 + at % 8 == zpos)))
        def _():
            greet(device(at // 8, core * 8 + at % 8, ypos))

        return carry

    lax.fori_loop(0, 16, greet_z, 0)

    def greet_key(step, carry):
        greet((core, (key + step) % 8, col))
        return carry

    lax.fori_loop(1, 8, greet_key, 0)

    loads = [
        pltpu.make_async_copy(src, dst, in_sem.at[at])
        for at, (src, dst) in enumerate(
            (
                (gain_hbm, gain_v), (win_hbm, win_v), (bin_hbm, bin_v), (woutt_hbm, woutt_v),
                (table_hbm, table_v), (bucket_hbm, bucket_v), (mask_hbm, mask_v), (q_hbm, q_v),
                (out_hbm, out_v), (dout_hbm, dout_v), (norm_hbm, norm_v),
            )
        )
    ]
    for load in loads:
        load.start()

    def x_load(pair):
        return pltpu.make_async_copy(x_hbm.at[pl.ds(pair * 2, 2)], x_v.at[pl.ds(pair * 2, 2)], x_sem.at[pair])

    for pair in range(8):
        x_load(pair).start()

    k_load = pltpu.make_async_copy(k_hbm.at[0], kv_v.at[slot, pl.ds(0, 32)], kv_sem.at[0])
    v_load = pltpu.make_async_copy(v_hbm.at[0], kv_v.at[slot, pl.ds(32, 32)], kv_sem.at[1])

    @pl.when(is_home)
    def _():
        k_load.start()
        v_load.start()

    for load in loads:
        load.wait()

    sel_row = iota((32, 32), 0)
    part_at, head_at = sel_row // 8, sel_row % 8
    head_of = 2 * (8 * (part_at // 2) + head_at) + part_at % 2
    select = ones_where(iota((32, 32), 1) == head_of)
    woutt = woutt_v[...]
    wmix_v[...] = dot(select, woutt).astype(BF16)
    tab_v[...] = dot(select, table_v[...].T).astype(BF16)
    row64 = iota((64, 32), 0)
    part64, head64 = row64 // 16, row64 % 8
    head_of64 = 2 * (8 * (part64 // 2) + head64) + part64 % 2
    spread = dot(ones_where(iota((64, 32), 1) == head_of64), woutt).T
    parity = (iota((256, 64), 1) // 8) % 2
    w2_v[0:256, :] = jnp.where(parity == 0, spread, 0.0).astype(BF16)
    w2_v[256:512, :] = jnp.where(parity == 1, spread, 0.0).astype(BF16)
    win_t = win_v[...].astype(F32).T
    zero = jnp.zeros((256, 64), F32)
    w1_v[0:256, :] = jnp.concatenate([win_t, zero], axis=1).astype(BF16)
    w1_v[256:512, :] = jnp.concatenate([zero, win_t], axis=1).astype(BF16)
    gain_col = column(gain_v[...])
    bin_col = column(bin_v[...])

    dout_f = dout_v[0].astype(F32)
    delta = jnp.sum(dout_f * out_v[0].astype(F32), axis=0, keepdims=True)
    n0, n1, n2 = pieces(norm_v[...])
    d0, d1, d2 = pieces(delta)
    sub = iota((64, 512), 0)
    extra = jnp.zeros((64, 512), F32)
    for at, piece in enumerate((n0, n1, n2, d0, d1, d2)):
        extra = jnp.where(sub == at, jnp.broadcast_to(piece, (64, 512)), extra)
    packed = jnp.concatenate([q_v[0].astype(F32), dout_f, extra], axis=0)
    qstage[...] = packed.T.astype(BF16).reshape(16, 32, 128)

    def q_copy(at):
        return pltpu.make_async_remote_copy(
            src_ref=qstage.at[at], dst_ref=qrecv.at[slot * 2 + core], send_sem=q_send.at[at],
            recv_sem=q_recv.at[slot * 2 + core], device_id=device(home, at, ypos), device_id_type=MESH,
        )

    def q_arrival(at):
        return pltpu.make_async_remote_copy(
            src_ref=qstage.at[0], dst_ref=qrecv.at[at], send_sem=q_send.at[0],
            recv_sem=q_recv.at[at], device_id=device(at % 2, core * 8 + at // 2, ypos), device_id_type=MESH,
        )

    def ag_copy(at, way, where):
        return pltpu.make_async_remote_copy(
            src_ref=kv_v.at[at], dst_ref=kv_v.at[at], send_sem=ag_send.at[way, at],
            recv_sem=ag_recv.at[at], device_id=where, device_id_type=MESH,
        )

    def ag_step(step):
        from_left = (zpos + 16 - step) % 16
        from_right = (zpos + step) % 16

        @pl.when(jnp.logical_and(step <= 8, from_left // 8 == core))
        def _():
            ag_copy(from_left % 8, 0, right).wait_recv()

            @pl.when(step < 8)
            def _():
                ag_copy(from_left % 8, 0, right).start()

        @pl.when(jnp.logical_and(step <= 7, from_right // 8 == core))
        def _():
            ag_copy(from_right % 8, 1, left).wait_recv()

            @pl.when(step < 7)
            def _():
                ag_copy(from_right % 8, 1, left).start()

    def ag_drain(step, carry):
        from_left = (zpos + 16 - step) % 16
        from_right = (zpos + step) % 16

        @pl.when(jnp.logical_and(step < 8, from_left // 8 == core))
        def _():
            ag_copy(from_left % 8, 0, right).wait_send()

        @pl.when(jnp.logical_and(step < 7, from_right // 8 == core))
        def _():
            ag_copy(from_right % 8, 1, left).wait_send()

        return carry

    def bias_copy(step, pair):
        where, part = quad(step)
        return pltpu.make_async_remote_copy(
            src_ref=bias_out.at[part, pair], dst_ref=bias_in.at[mine, pair], send_sem=b_send.at[step],
            recv_sem=b_recv.at[mine], device_id=where, device_id_type=MESH,
        )

    def bias_all(step):
        where, part = quad(step)
        return pltpu.make_async_remote_copy(
            src_ref=bias_out.at[part], dst_ref=bias_in.at[part], send_sem=b_send.at[step],
            recv_sem=b_recv.at[part], device_id=where, device_id_type=MESH,
        )

    def forward_pair(pair):
        x_load(pair).wait()
        mats = []
        for r in range(2):
            values = x_v[pair * 2 + r].astype(F32)
            mean = jnp.sum(values, axis=0, keepdims=True) * (1.0 / 64.0)
            centre = values - mean
            inv_std = lax.rsqrt(jnp.sum(centre * centre, axis=0, keepdims=True) * (1.0 / 64.0) + 1e-05)
            stat_v[pair * 2 + r, 0:1, :] = mean
            stat_v[pair * 2 + r, 1:2, :] = inv_std
            mats.append((centre * inv_std * gain_col).astype(BF16))
        pre = dot(w1_v[...], jnp.concatenate(mats, axis=0))
        mixes = []
        for r in range(2):
            gelu_val, gelu_slope = gelu_parts(pre[r * 256:(r + 1) * 256] + bin_col)
            slope_v[pair * 2 + r] = gelu_slope.astype(BF16)
            hidden = gelu_val.astype(BF16)
            onehot = ones_where(bucket_v[pl.ds(pair * 2 + r, 1), :] == iota((32, 1024), 0))
            mixes.append(dot(wmix_v[...], hidden) + dot(tab_v[...], onehot))
        for part in range(4):
            rows = [mix[part * 8:(part + 1) * 8] for mix in mixes]
            bias_out[part, pair] = jnp.concatenate(rows, axis=0).astype(BF16)

    forward_pair(0)

    @pl.when(is_home)
    def _():
        pl.semaphore_wait(barrier, 42)

    @pl.when(jnp.logical_not(is_home))
    def _():
        pl.semaphore_wait(barrier, 44)

    @pl.when(is_home)
    def _():
        k_load.wait()
        v_load.wait()
        ag_copy(slot, 0, right).start()
        ag_copy(slot, 1, left).start()
        qrecv[slot * 2 + core] = qstage[zpos]

    def q_start(at, carry):
        @pl.when(jnp.logical_not(jnp.logical_and(is_home, at == zpos)))
        def _():
            q_copy(at).start()

        return carry

    lax.fori_loop(0, 16, q_start, 0)
    for step in (1, 2, 3):
        bias_copy(step, 0).start()

    def forward_body(pair, carry):
        forward_pair(pair)
        for step in (1, 2, 3):
            bias_copy(step, pair).start()
        ag_step(pair)
        return carry

    lax.fori_loop(1, 8, forward_body, 0)

    def q_wait(at, carry):
        @pl.when(jnp.logical_not(jnp.logical_and(at % 2 == core, core * 8 + at // 2 == zpos)))
        def _():
            q_arrival(at).wait_recv()

        return carry

    lax.fori_loop(0, 16, q_wait, 0)
    arrived = qrecv[...].reshape(512, 128)
    row_a, row_b = iota((512, 512), 0), iota((512, 512), 1)
    order = ones_where(jnp.logical_and(row_a // 8 == row_b % 64, row_a % 8 == row_b // 64))
    by_row = dot(order, arrived).astype(BF16)
    lane, spot = iota((128, 256), 0), iota((128, 256), 1)
    own_head = iota((512, 256), 0) % 8 == iota((512, 256), 1) // 32
    qblk_v[...] = jnp.where(own_head, dot(by_row, ones_where(lane == spot % 32)), 0.0).astype(BF16)
    doblk_v[...] = jnp.where(own_head, dot(by_row, ones_where(lane == 32 + spot % 32)), 0.0).astype(BF16)
    wide = iota((128, 128), 0)
    norm_b[...] = dot(by_row, ones_where(jnp.logical_and(wide >= 64, wide < 67)))
    delta_b[...] = dot(by_row, ones_where(jnp.logical_and(wide >= 67, wide < 70)))

    ag_step(8)
    live = mask_v[...] == 1
    keys = kv_v[:, 0:32, :].reshape(256, 1024)
    values = kv_v[:, 32:64, :].reshape(256, 1024)

    def ds_copy(step):
        where, part = quad(step)
        return pltpu.make_async_remote_copy(
            src_ref=ds_all.at[part], dst_ref=ds_in.at[mine], send_sem=d_send.at[step],
            recv_sem=d_recv.at[mine], device_id=where, device_id_type=MESH,
        )

    def ds_arrival(step):
        where, part = quad(step)
        return pltpu.make_async_remote_copy(
            src_ref=ds_all.at[part], dst_ref=ds_in.at[part], send_sem=d_send.at[step],
            recv_sem=d_recv.at[part], device_id=where, device_id_type=MESH,
        )

    for step in (1, 2, 3, 0):
        _, part = quad(step)
        if step:
            bias_all(step).wait_recv()
            bias = bias_in[part]
        else:
            bias = bias_out[part]
        rows = pl.ds(pl.multiple_of(part * 128, 128), 128)
        scores = dot(qblk_v[rows, :], keys) * score_scale + bias.reshape(128, 1024).astype(F32)
        shift = jnp.concatenate([norm_b[rows, :]] * 8, axis=1)
        probs = jnp.where(live, jnp.exp(scores - shift), 0.0)
        probs_v[rows, :] = probs.astype(BF16)
        less = jnp.concatenate([delta_b[rows, :]] * 8, axis=1)
        dscores = (probs * (dot(doblk_v[rows, :], values) - less)).astype(BF16)
        ds_all[part] = dscores
        if step:
            ds_copy(step).start()
        else:
            ds_in[part] = dscores

    ds_flat = ds_all[...].reshape(512, 1024)
    dkv_v[:, 0:32, :] = dot(qblk_v[...].T, ds_flat).reshape(8, 32, 1024)
    dkv_v[:, 32:64, :] = dot(doblk_v[...].T, probs_v[...]).reshape(8, 32, 1024)

    def rs_plus(step):
        return pltpu.make_async_remote_copy(
            src_ref=rsp_send.at[step], dst_ref=rsp_recv.at[step], send_sem=rp_send.at[step],
            recv_sem=rp_recv.at[step], device_id=right, device_id_type=MESH,
        )

    def rs_minus(step):
        return pltpu.make_async_remote_copy(
            src_ref=rsm_send.at[step], dst_ref=rsm_recv.at[step], send_sem=rm_send.at[step],
            recv_sem=rm_recv.at[step], device_id=left, device_id_type=MESH,
        )

    def to_right(step):
        return (zpos + 8 - step) % 16

    def to_left(step):
        return (zpos + 9 + step) % 16

    @pl.when(to_right(0) // 8 == core)
    def _():
        rsp_send[0] = dkv_v[to_right(0) % 8].astype(BF16)
        rs_plus(0).start()

    @pl.when(to_left(0) // 8 == core)
    def _():
        rsm_send[0] = dkv_v[to_left(0) % 8].astype(BF16)
        rs_minus(0).start()

    def rs_step(step):
        @pl.when(jnp.logical_and(step < 8, to_right(step) // 8 == core))
        def _():
            rs_plus(step - 1).wait_recv()
            rsp_send[step] = (rsp_recv[step - 1].astype(F32) + dkv_v[to_right(step) % 8]).astype(BF16)
            rs_plus(step).start()

        @pl.when(jnp.logical_and(step < 7, to_left(step) // 8 == core))
        def _():
            rs_minus(step - 1).wait_recv()
            rsm_send[step] = (rsm_recv[step - 1].astype(F32) + dkv_v[to_left(step) % 8]).astype(BF16)
            rs_minus(step).start()

    dq_full = lax.dot_general(ds_flat, keys, (((1,), (1,)), ((), ())), preferred_element_type=F32)
    dq_full = jnp.where(own_head, dq_full, 0.0)
    dq_fold = dq_full[:, 0:128] + dq_full[:, 128:256]
    dq_fold = dq_fold + pltpu.roll(dq_fold, 64, 1)
    dq_fold = dq_fold + pltpu.roll(dq_fold, 32, 1)
    group = iota((512, 128), 1) // 32
    h0, h1, h2 = pieces(dq_fold)
    dq_split = jnp.where(group == 0, h0, jnp.where(group == 1, h1, jnp.where(group == 2, h2, 0.0))).astype(BF16)
    back = ones_where(jnp.logical_and(row_b // 8 == row_a % 64, row_b % 8 == row_a // 64))
    dq_head = dot(back, dq_split)
    dq_head = dq_head + pltpu.roll(dq_head, 64, 1)
    dq_head = dq_head + pltpu.roll(dq_head, 32, 1)
    dq_head = dq_head.reshape(16, 32, 128)
    group8 = iota((16, 8, 128), 2) // 32
    dense = dq_head[:, 0:8, :]
    for at in range(1, 4):
        dense = jnp.where(group8 == at, dq_head[:, at * 8:(at + 1) * 8, :], dense)
    dq_send[...] = dense

    def p1_copy(at):
        return pltpu.make_async_remote_copy(
            src_ref=dq_send.at[at], dst_ref=dq_recv.at[zpos], send_sem=p1_send.at[at],
            recv_sem=p1_recv.at[zpos], device_id=device(at % 2, core * 8 + at // 2, ypos), device_id_type=MESH,
        )

    def p1_arrival(at):
        return pltpu.make_async_remote_copy(
            src_ref=dq_send.at[0], dst_ref=dq_recv.at[at], send_sem=p1_send.at[0],
            recv_sem=p1_recv.at[at], device_id=device(home, at, ypos), device_id_type=MESH,
        )

    def p1_start(at, carry):
        @pl.when(jnp.logical_not(jnp.logical_and(at % 2 == core, core * 8 + at // 2 == zpos)))
        def _():
            p1_copy(at).start()

        return carry

    lax.fori_loop(0, 16, p1_start, 0)

    @pl.when(is_home)
    def _():
        dq_recv[zpos] = dq_send[slot * 2 + core]

    def p2_copy(step):
        return pltpu.make_async_remote_copy(
            src_ref=dq_recv, dst_ref=dq_peers.at[key], send_sem=p2_send.at[step],
            recv_sem=p2_recv.at[key], device_id=(core, (key + step) % 8, col), device_id_type=MESH,
        )

    def p2_arrival(step):
        peer = (key + step) % 8
        return pltpu.make_async_remote_copy(
            src_ref=dq_recv, dst_ref=dq_peers.at[peer], send_sem=p2_send.at[step],
            recv_sem=p2_recv.at[peer], device_id=(core, peer, col), device_id_type=MESH,
        )

    def phase_two():
        def p1_wait(at, carry):
            @pl.when(jnp.logical_not(jnp.logical_and(is_home, at == zpos)))
            def _():
                p1_arrival(at).wait_recv()

            return carry

        lax.fori_loop(0, 16, p1_wait, 0)
        dq_peers[key] = dq_recv[...]

        def p2_start(step, carry):
            p2_copy(step).start()
            return carry

        lax.fori_loop(1, 8, p2_start, 0)

    for step in (1, 2, 3):
        ds_arrival(step).wait_recv()

    win = win_v[...]

    def gp_copy(pair):
        return pltpu.make_async_copy(gp_v.at[pl.ds(pair * 2, 2)], gp_hbm.at[pl.ds(pair * 2, 2)], gp_sem.at[pair])

    def backward_pair(pair):
        at = pl.ds(pl.multiple_of(pair * 16, 16), 16)
        dhidden = dot(w2_v[...], ds_in[:, at, :].reshape(64, 1024))
        for r in range(2):
            row = pair * 2 + r
            dpre = (dhidden[r * 256:(r + 1) * 256] * slope_v[row].astype(F32)).astype(BF16)
            dunit = dot(win, dpre) * gain_col
            inv_std = stat_v[row, 1:2, :]
            unit = (x_v[row].astype(F32) - stat_v[row, 0:1, :]) * inv_std
            first = jnp.sum(dunit, axis=0, keepdims=True) * (1.0 / 64.0)
            second = jnp.sum(dunit * unit, axis=0, keepdims=True) * (1.0 / 64.0)
            gp_v[row] = (inv_std * (dunit - first - unit * second)).astype(BF16)
        gp_copy(pair).start()

    def backward_body(pair, carry):
        backward_pair(pair)
        rs_step(pair + 1)

        @pl.when(pair == 3)
        def _():
            phase_two()

        return carry

    lax.fori_loop(0, 7, backward_body, 0)
    backward_pair(7)

    sibling, _ = quad(2)

    def f_copy():
        return pltpu.make_async_remote_copy(
            src_ref=gkv_v, dst_ref=gkv_v, send_sem=f_send, recv_sem=f_recv,
            device_id=sibling, device_id_type=MESH,
        )

    @pl.when(is_home)
    def _():
        rs_plus(7).wait_recv()
        rs_minus(6).wait_recv()
        total = dkv_v[slot] + rsp_recv[7].astype(F32) + rsm_recv[6].astype(F32)
        gkv_v[0:32, :] = (total[0:32] * score_scale).astype(BF16)
        gkv_v[32:64, :] = total[32:64].astype(BF16)
        f_copy().start()

    def p2_wait(step, carry):
        p2_arrival(step).wait_recv()
        return carry

    lax.fori_loop(1, 8, p2_wait, 0)
    total_q = dq_peers[0]
    for at in range(1, 8):
        total_q = total_q + dq_peers[at]
    final_q = (total_q.reshape(128, 128) * score_scale).astype(BF16).astype(F32).T.astype(BF16)
    lane_a, lane_b = iota((128, 512), 0), iota((128, 512), 1)
    grad_q = jnp.zeros((32, 512), F32)
    for at in range(4):
        place = jnp.logical_and(
            lane_a // 8 == lane_b // 32,
            jnp.logical_and(lane_a % 8 == lane_b % 8, (lane_b // 8) % 4 == at),
        )
        grad_q = grad_q + dot(final_q[at * 32:(at + 1) * 32, :], ones_where(place))
    gq_v[...] = grad_q.astype(BF16)
    gq_copy = pltpu.make_async_copy(gq_v, gq_hbm.at[0], o_sem.at[0])
    gq_copy.start()

    @pl.when(jnp.logical_not(is_home))
    def _():
        f_copy().wait_recv()

    gk_copy = pltpu.make_async_copy(gkv_v.at[pl.ds(0, 32)], gk_hbm.at[0], o_sem.at[1])
    gv_copy = pltpu.make_async_copy(gkv_v.at[pl.ds(32, 32)], gv_hbm.at[0], o_sem.at[2])
    gk_copy.start()
    gv_copy.start()

    @pl.when(is_home)
    def _():
        f_copy().wait_send()
        ag_copy(slot, 0, right).wait_send()
        ag_copy(slot, 1, left).wait_send()

    lax.fori_loop(1, 8, ag_drain, 0)

    def z_drain(at, carry):
        @pl.when(jnp.logical_not(jnp.logical_and(is_home, at == zpos)))
        def _():
            q_copy(at).wait_send()

        @pl.when(jnp.logical_not(jnp.logical_and(at % 2 == core, core * 8 + at // 2 == zpos)))
        def _():
            p1_copy(at).wait_send()

        return carry

    lax.fori_loop(0, 16, z_drain, 0)
    for step in (1, 2, 3):
        bias_all(step).wait_send()
        ds_copy(step).wait_send()

    def rs_drain(step, carry):
        @pl.when(to_right(step) // 8 == core)
        def _():
            rs_plus(step).wait_send()

        @pl.when(jnp.logical_and(step < 7, to_left(step) // 8 == core))
        def _():
            rs_minus(step).wait_send()

        return carry

    lax.fori_loop(0, 8, rs_drain, 0)

    def last_drain(step, carry):
        p2_copy(step).wait_send()
        return carry

    lax.fori_loop(1, 8, last_drain, 0)

    def gp_drain(pair, carry):
        gp_copy(pair).wait()
        return carry

    lax.fori_loop(0, 8, gp_drain, 0)
    gq_copy.wait()
    gk_copy.wait()
    gv_copy.wait()


def per_device(
    pair_feats, bucket_ids, ln_gain, w_in, b_in, w_out, bucket_table, key_mask,
    q_heads, k_heads, v_heads, out_heads, dout_heads, log_norm,
):
    any_space = pl.BlockSpec(memory_space=pl.ANY)
    vmem = pltpu.VMEM
    dma = pltpu.SemaphoreType.DMA
    return pl.pallas_call(
        kernel,
        out_shape=(
            jax.ShapeDtypeStruct((16, 64, 1024), BF16),
            jax.ShapeDtypeStruct((1, 32, 512), BF16),
            jax.ShapeDtypeStruct((1, 32, 1024), BF16),
            jax.ShapeDtypeStruct((1, 32, 1024), BF16),
        ),
        in_specs=[any_space] * 14,
        out_specs=(any_space,) * 4,
        scratch_shapes=[
            vmem((16, 64, 1024), BF16),
            vmem((16, 1024), jnp.int32),
            vmem((1, 64), F32),
            vmem((64, 256), BF16),
            vmem((1, 256), F32),
            vmem((32, 256), BF16),
            vmem((32, 32), BF16),
            vmem((1, 1024), jnp.int32),
            vmem((1, 32, 512), BF16),
            vmem((1, 32, 512), BF16),
            vmem((1, 32, 512), BF16),
            vmem((1, 512), F32),
            vmem((16, 64, 1024), BF16),
            vmem((32, 512), BF16),
            vmem((64, 1024), BF16),
            vmem((16, 256, 1024), BF16),
            vmem((16, 2, 1024), F32),
            vmem((8, 64, 1024), BF16),
            vmem((4, 8, 16, 1024), BF16),
            vmem((4, 8, 16, 1024), BF16),
            vmem((4, 128, 1024), BF16),
            vmem((4, 128, 1024), BF16),
            vmem((512, 1024), BF16),
            vmem((16, 32, 128), BF16),
            vmem((16, 32, 128), BF16),
            vmem((512, 256), BF16),
            vmem((512, 256), BF16),
            vmem((512, 128), F32),
            vmem((512, 128), F32),
            vmem((8, 64, 1024), F32),
            vmem((8, 64, 1024), BF16),
            vmem((8, 64, 1024), BF16),
            vmem((7, 64, 1024), BF16),
            vmem((7, 64, 1024), BF16),
            vmem((16, 8, 128), F32),
            vmem((16, 8, 128), F32),
            vmem((8, 16, 8, 128), F32),
            vmem((512, 128), BF16),
            vmem((512, 64), BF16),
            vmem((32, 256), BF16),
            vmem((32, 32), BF16),
            dma((11,)), dma((8,)), dma((2,)), dma((8,)), dma((3,)),
            dma((2, 8)), dma((8,)), dma((16,)), dma((16,)), dma((4,)), dma((4,)), dma((4,)), dma((4,)),
            dma((8,)), dma((8,)), dma((7,)), dma((7,)), dma, dma,
            dma((16,)), dma((16,)), dma((8,)), dma((8,)),
        ],
        compiler_params=pltpu.CompilerParams(
            collective_id=0, has_side_effects=True, vmem_limit_bytes=56 * 2**20
        ),
        name="pair_attention_backward",
    )(
        pair_feats, bucket_ids, ln_gain.reshape(1, 64), w_in, b_in.reshape(1, 256), w_out.T,
        bucket_table, key_mask.reshape(1, 1024), q_heads, k_heads, v_heads, out_heads, dout_heads, log_norm,
    )


def solution(mesh):
    return jax.shard_map(
        per_device,
        mesh=mesh,
        in_specs=(
            P(("query", "heads"), None, "key"),
            P(("query", "heads"), "key"),
            P(),
            P(),
            P(),
            P(),
            P(),
            P("key"),
            P("heads", None, "query"),
            P("heads", None, "key"),
            P("heads", None, "key"),
            P("heads", None, "query"),
            P("heads", None, "query"),
            P("heads", "query"),
        ),
        out_specs=(
            P(("query", "heads"), None, "key"),
            P("heads", None, "query"),
            P("heads", None, "key"),
            P("heads", None, "key"),
        ),
        check_vma=False,
    )
```

```python
import functools
import math

import jax
import jax.numpy as jnp
from jax import lax
from jax.experimental import pallas as pl
from jax.experimental.pallas import tpu as pltpu
from jax.sharding import PartitionSpec as P

F32 = jnp.float32
BF16 = jnp.bfloat16
MESH = pl.DeviceIdType.MESH


def dot(lhs, rhs):
    return jnp.dot(lhs, rhs, preferred_element_type=F32)


def iota(shape, axis):
    return lax.broadcasted_iota(jnp.int32, shape, axis)


def ones_where(cond):
    return jnp.where(cond, 1.0, 0.0).astype(BF16)


def column(row):
    size = row.shape[1]
    diag = iota((size, size), 0) == iota((size, size), 1)
    return jnp.sum(jnp.where(diag, jnp.broadcast_to(row, (size, size)), 0.0), axis=1, keepdims=True)


def pieces(value):
    first = value.astype(BF16).astype(F32)
    second = (value - first).astype(BF16).astype(F32)
    third = (value - first - second).astype(BF16).astype(F32)
    return first, second, third


def gelu_parts(pre_act):
    cdf_val = 0.5 * (1.0 + lax.erf(pre_act * (1.0 / math.sqrt(2.0))))
    density = jnp.exp(-0.5 * pre_act * pre_act) * (1.0 / math.sqrt(2.0 * math.pi))
    return pre_act * cdf_val, cdf_val + pre_act * density


def kernel(
    x_hbm, bucket_hbm, gain_hbm, win_hbm, bin_hbm, woutt_hbm, table_hbm, mask_hbm,
    q_hbm, k_hbm, v_hbm, out_hbm, dout_hbm, norm_hbm,
    gp_hbm, gq_hbm, gk_hbm, gv_hbm,
    x_v, bucket_v, gain_v, win_v, bin_v, woutt_v, table_v, mask_v,
    q_v, out_v, dout_v, norm_v,
    gp_v, gq_v, gkv_v,
    slope_v, stat_v, kv_v, bias_out, bias_in, ds_all, ds_in, probs_v, probs_f,
    qstage, qrecv, qblk_v, doblk_v, norm_b, delta_b, dkv_v,
    rsp_send, rsp_recv, rsm_send, rsm_recv,
    dq_send, dq_recv, dq_peers, w1_v, w2_v, wmix_v, tab_v,
    in_sem, x_sem, kv_sem, gp_sem, o_sem,
    ag_send, ag_recv, q_send, q_recv, b_send, b_recv, d_send, d_recv,
    rp_send, rp_recv, rm_send, rm_recv, f_send, f_recv,
    p1_send, p1_recv, p2_send, p2_recv, round_one, round_two,
):
    core = lax.axis_index("query")
    key = lax.axis_index("key")
    col = lax.axis_index("heads")
    zpos = col // 2
    ypos = col % 2
    home = zpos // 8
    slot = zpos % 8
    mine = core * 2 + ypos
    is_home = home == core
    score_scale = 1.0 / math.sqrt(32.0)

    def device(core_at, z_at, y_at):
        return (core_at, key, z_at * 2 + y_at)

    def along(hops):
        return device(core, (zpos + 16 + hops) % 16, ypos)

    def along_x(hops):
        return (core, (key + 8 + 2 * hops) % 8, col)

    across_y = (core, key + 1 - 2 * (key % 2), col)

    def quad(step):
        core_at = (core + step // 2) % 2
        y_at = (ypos + step % 2) % 2
        return device(core_at, zpos, y_at), core_at * 2 + y_at

    barrier = pltpu.get_barrier_semaphore()

    def greet(where):
        pl.semaphore_signal(barrier, inc=1, device_id=where, device_id_type=MESH)

    for hops in (1, -1, 2, -2):
        greet(along(hops))
        greet(device(1 - core, (zpos + 16 + hops) % 16, ypos))
    for step in (1, 2, 3):
        greet(quad(step)[0])
    greet(along_x(1))
    greet(along_x(-1))
    greet(across_y)

    loads = [
        pltpu.make_async_copy(src, dst, in_sem.at[at])
        for at, (src, dst) in enumerate(
            (
                (gain_hbm, gain_v), (win_hbm, win_v), (bin_hbm, bin_v), (woutt_hbm, woutt_v),
                (table_hbm, table_v), (bucket_hbm, bucket_v), (mask_hbm, mask_v), (q_hbm, q_v),
                (out_hbm, out_v), (dout_hbm, dout_v), (norm_hbm, norm_v),
            )
        )
    ]
    for load in loads:
        load.start()

    def x_load(pair):
        return pltpu.make_async_copy(x_hbm.at[pl.ds(pair * 2, 2)], x_v.at[pl.ds(pair * 2, 2)], x_sem.at[pair])

    for pair in range(8):
        x_load(pair).start()

    k_load = pltpu.make_async_copy(k_hbm.at[0], kv_v.at[0, slot], kv_sem.at[0])
    v_load = pltpu.make_async_copy(v_hbm.at[0], kv_v.at[1, slot], kv_sem.at[1])

    @pl.when(is_home)
    def _():
        k_load.start()
        v_load.start()

    for load in loads:
        load.wait()

    sel_row = iota((32, 32), 0)
    part_at, head_at = sel_row // 8, sel_row % 8
    head_of = 2 * (8 * (part_at // 2) + head_at) + part_at % 2
    select = ones_where(iota((32, 32), 1) == head_of)
    woutt = woutt_v[...]
    wmix_v[...] = dot(select, woutt).astype(BF16)
    tab_v[...] = dot(select, table_v[...].T).astype(BF16)
    row64 = iota((64, 32), 0)
    part64, head64 = row64 // 16, row64 % 8
    head_of64 = 2 * (8 * (part64 // 2) + head64) + part64 % 2
    spread = dot(ones_where(iota((64, 32), 1) == head_of64), woutt).T
    parity = (iota((256, 64), 1) // 8) % 2
    w2_v[0:256, :] = jnp.where(parity == 0, spread, 0.0).astype(BF16)
    w2_v[256:512, :] = jnp.where(parity == 1, spread, 0.0).astype(BF16)
    win_t = win_v[...].astype(F32).T
    zero = jnp.zeros((256, 64), F32)
    w1_v[0:256, :] = jnp.concatenate([win_t, zero], axis=1).astype(BF16)
    w1_v[256:512, :] = jnp.concatenate([zero, win_t], axis=1).astype(BF16)
    gain_col = column(gain_v[...])
    bin_col = column(bin_v[...])

    dout_f = dout_v[0].astype(F32)
    delta = jnp.sum(dout_f * out_v[0].astype(F32), axis=0, keepdims=True)
    n0, n1, n2 = pieces(norm_v[...])
    d0, d1, d2 = pieces(delta)
    sub = iota((64, 512), 0)
    extra = jnp.zeros((64, 512), F32)
    for at, piece in enumerate((n0, n1, n2, d0, d1, d2)):
        extra = jnp.where(sub == at, jnp.broadcast_to(piece, (64, 512)), extra)
    packed = jnp.concatenate([q_v[0].astype(F32), dout_f, extra], axis=0)
    qstage[...] = packed.T.astype(BF16).reshape(16, 32, 128)

    def q_copy(at):
        return pltpu.make_async_remote_copy(
            src_ref=qstage.at[at], dst_ref=qrecv.at[slot * 2 + core], send_sem=q_send.at[at],
            recv_sem=q_recv.at[slot * 2 + core], device_id=device(home, at, ypos), device_id_type=MESH,
        )

    def q_arrival(at):
        return pltpu.make_async_remote_copy(
            src_ref=qstage.at[0], dst_ref=qrecv.at[at], send_sem=q_send.at[0],
            recv_sem=q_recv.at[at], device_id=device(at % 2, core * 8 + at // 2, ypos), device_id_type=MESH,
        )

    def ag_copy(half, at, way, hops):
        return pltpu.make_async_remote_copy(
            src_ref=kv_v.at[half, at], dst_ref=kv_v.at[half, at],
            send_sem=ag_send.at[half, way * 2 + hops - 1, at],
            recv_sem=ag_recv.at[half, at], device_id=along(hops - 2 * hops * way), device_id_type=MESH,
        )

    def ag_source(way, hops):
        return (zpos + 16 - hops + 2 * hops * way) % 16

    def ag_forward(half, hops, ending=False):
        for way in range(2):
            source = ag_source(way, hops)

            @pl.when(source // 8 == core)
            def _():
                onward = [ag_copy(half, source % 8, way, hop) for hop in ((1,) if way == 1 and hops == 6 else (2, 1))]
                if ending:
                    for copy in onward:
                        copy.wait_send()
                else:
                    onward[0].wait_recv()
                    for copy in onward:
                        copy.start()

    def ag_finish(half):
        for way, hops in ((0, 1), (0, 3), (0, 5), (0, 7), (0, 8), (1, 1), (1, 3), (1, 5), (1, 7)):
            source = ag_source(way, hops)

            @pl.when(source // 8 == core)
            def _():
                ag_copy(half, source % 8, way, 1).wait_recv()

    def bias_copy(step, pair):
        where, part = quad(step)
        return pltpu.make_async_remote_copy(
            src_ref=bias_out.at[part, pair], dst_ref=bias_in.at[mine, pair], send_sem=b_send.at[step],
            recv_sem=b_recv.at[mine], device_id=where, device_id_type=MESH,
        )

    def bias_all(step):
        where, part = quad(step)
        return pltpu.make_async_remote_copy(
            src_ref=bias_out.at[part], dst_ref=bias_in.at[part], send_sem=b_send.at[step],
            recv_sem=b_recv.at[part], device_id=where, device_id_type=MESH,
        )

    def forward_pair(pair):
        x_load(pair).wait()
        mats = []
        for r in range(2):
            values = x_v[pair * 2 + r].astype(F32)
            mean = jnp.sum(values, axis=0, keepdims=True) * (1.0 / 64.0)
            centre = values - mean
            inv_std = lax.rsqrt(jnp.sum(centre * centre, axis=0, keepdims=True) * (1.0 / 64.0) + 1e-05)
            stat_v[pair * 2 + r, 0:1, :] = mean
            stat_v[pair * 2 + r, 1:2, :] = inv_std
            mats.append((centre * inv_std * gain_col).astype(BF16))
        pre = dot(w1_v[...], jnp.concatenate(mats, axis=0))
        mixes = []
        for r in range(2):
            gelu_val, gelu_slope = gelu_parts(pre[r * 256:(r + 1) * 256] + bin_col)
            slope_v[pair * 2 + r] = gelu_slope.astype(BF16)
            hidden = gelu_val.astype(BF16)
            onehot = ones_where(bucket_v[pl.ds(pair * 2 + r, 1), :] == iota((32, 1024), 0))
            mixes.append(dot(wmix_v[...], hidden) + dot(tab_v[...], onehot))
        for part in range(4):
            rows = [mix[part * 8:(part + 1) * 8] for mix in mixes]
            bias_out[part, pair] = jnp.concatenate(rows, axis=0).astype(BF16)

    def bias_send(pair):
        for step in (1, 2, 3):
            bias_copy(step, pair).start()

    def forward_only(pair, carry):
        forward_pair(pair)
        return carry

    lax.fori_loop(0, 2, forward_only, 0)
    pl.semaphore_wait(barrier, 14)

    @pl.when(is_home)
    def _():
        k_load.wait()
        v_load.wait()
        for half in range(2):
            for hops in (2, 1):
                ag_copy(half, slot, 0, hops).start()
                ag_copy(half, slot, 1, hops).start()

    for where in (along(2), along(-2), along_x(1), along_x(-1)):
        pl.semaphore_signal(round_one, inc=1, device_id=where, device_id_type=MESH)
    bias_send(0)
    bias_send(1)

    def q_start(at, carry):
        @pl.when(jnp.logical_not(jnp.logical_and(is_home, at == zpos)))
        def _():
            q_copy(at).start()

        return carry

    def forward_body(pair, carry):
        forward_pair(pair)
        bias_send(pair)

        @pl.when(pair == 3)
        def _():
            pl.semaphore_wait(round_one, 4)
            for where in (along(4), along(-4), across_y):
                pl.semaphore_signal(round_two, inc=1, device_id=where, device_id_type=MESH)
            ag_forward(0, 2)

        @pl.when(pair == 4)
        def _():
            ag_forward(1, 2)

        @pl.when(pair == 5)
        def _():
            pl.semaphore_wait(round_two, 3)
            lax.fori_loop(0, 16, q_start, 0)
            ag_forward(0, 4)

        @pl.when(pair == 6)
        def _():
            ag_forward(1, 4)

        return carry

    lax.fori_loop(2, 8, forward_body, 0)

    @pl.when(is_home)
    def _():
        qrecv[slot * 2 + core] = qstage[zpos]

    ag_forward(0, 6)

    def q_wait(at, carry):
        @pl.when(jnp.logical_not(jnp.logical_and(at % 2 == core, core * 8 + at // 2 == zpos)))
        def _():
            q_arrival(at).wait_recv()

        return carry

    lax.fori_loop(0, 16, q_wait, 0)
    arrived = qrecv[...].reshape(512, 128)
    row_a, row_b = iota((512, 512), 0), iota((512, 512), 1)
    order = ones_where(jnp.logical_and(row_a // 8 == row_b % 64, row_a % 8 == row_b // 64))
    by_row = dot(order, arrived).astype(BF16)
    lane, spot = iota((128, 256), 0), iota((128, 256), 1)
    own_head = iota((512, 256), 0) % 8 == iota((512, 256), 1) // 32
    qblk_v[...] = jnp.where(own_head, dot(by_row, ones_where(lane == spot % 32)), 0.0).astype(BF16)
    doblk_v[...] = jnp.where(own_head, dot(by_row, ones_where(lane == 32 + spot % 32)), 0.0).astype(BF16)
    wide = iota((128, 128), 0)
    norm_b[...] = dot(by_row, ones_where(jnp.logical_and(wide >= 64, wide < 67)))
    delta_b[...] = dot(by_row, ones_where(jnp.logical_and(wide >= 67, wide < 70)))

    ag_forward(1, 6)
    live = mask_v[...] == 1
    ag_finish(0)
    keys = kv_v[0].reshape(256, 1024)

    for step in (1, 2, 3, 0):
        _, part = quad(step)
        if step:
            bias_all(step).wait_recv()
            bias = bias_in[part]
        else:
            bias = bias_out[part]
        rows = pl.ds(pl.multiple_of(part * 128, 128), 128)
        scores = dot(qblk_v[rows, :], keys) * score_scale + bias.reshape(128, 1024).astype(F32)
        shift = jnp.concatenate([norm_b[rows, :]] * 8, axis=1)
        probs = jnp.where(live, jnp.exp(scores - shift), 0.0)
        probs_f[rows, :] = probs
        probs_v[rows, :] = probs.astype(BF16)
    dkv_v[:, 32:64, :] = dot(doblk_v[...].T, probs_v[...]).reshape(8, 32, 1024)

    def rs_copy(way, far, half):
        hops = 2 if far == 8 or far % 2 == 0 else 1
        send, recv, s_sem, r_sem = (
            (rsp_send, rsp_recv, rp_send, rp_recv), (rsm_send, rsm_recv, rm_send, rm_recv)
        )[way]
        return pltpu.make_async_remote_copy(
            src_ref=send.at[far - 1, half], dst_ref=recv.at[far - 1, half], send_sem=s_sem.at[far - 1, half],
            recv_sem=r_sem.at[far - 1, half], device_id=along(-hops if way else hops), device_id_type=MESH,
        )

    def rs_dest(way, far):
        return (zpos + 16 - far if way else zpos + far) % 16

    def rs_part(far, half, way):
        dest = rs_dest(way, far)
        send, recv = ((rsp_send, rsp_recv), (rsm_send, rsm_recv))[way]
        last = 7 if way else 8

        @pl.when(dest // 8 == core)
        def _():
            total = dkv_v[dest % 8, half * 32:half * 32 + 32, :]
            if far in (2, 4, 6):
                for other in (far + 1, far + 2):
                    if other <= last:
                        rs_copy(way, other, half).wait_recv()
                        total = total + recv[other - 1, half].astype(F32)
            send[far - 1, half] = total.astype(BF16)
            rs_copy(way, far, half).start()

    def rs_raw(half):
        for far in (8, 7, 5, 3, 1):
            for way in range(2):
                if not (way == 1 and far == 8):
                    rs_part(far, half, way)

    def rs_sum(far, half):
        for way in range(2):
            rs_part(far, half, way)

    rs_raw(1)
    ag_finish(1)
    values = kv_v[1].reshape(256, 1024)

    def ds_copy(step, piece):
        where, part = quad(step)
        at = pl.ds(piece * 32, 32)
        return pltpu.make_async_remote_copy(
            src_ref=ds_all.at[part, at], dst_ref=ds_in.at[mine, at], send_sem=d_send.at[step, piece],
            recv_sem=d_recv.at[mine, piece], device_id=where, device_id_type=MESH,
        )

    def ds_arrival(step, piece):
        where, part = quad(step)
        at = pl.ds(pl.multiple_of(piece * 32, 32), 32)
        return pltpu.make_async_remote_copy(
            src_ref=ds_all.at[part, at], dst_ref=ds_in.at[part, at], send_sem=d_send.at[step, piece],
            recv_sem=d_recv.at[part, piece], device_id=where, device_id_type=MESH,
        )

    for step in (1, 3, 2, 0):
        _, part = quad(step)
        rows = pl.ds(pl.multiple_of(part * 128, 128), 128)
        less = jnp.concatenate([delta_b[rows, :]] * 8, axis=1)
        dscores = (probs_f[rows, :] * (dot(doblk_v[rows, :], values) - less)).astype(BF16)
        ds_all[part] = dscores
        if not step:
            ds_in[part] = dscores
    for piece in range(4):
        for step in (1, 3, 2):
            ds_copy(step, piece).start()
    ds_flat = ds_all[...].reshape(512, 1024)
    dkv_v[:, 0:32, :] = dot(qblk_v[...].T, ds_flat).reshape(8, 32, 1024)
    rs_raw(0)

    dq_full = lax.dot_general(ds_flat, keys, (((1,), (1,)), ((), ())), preferred_element_type=F32)
    dq_full = jnp.where(own_head, dq_full, 0.0)
    dq_fold = dq_full[:, 0:128] + dq_full[:, 128:256]
    dq_fold = dq_fold + pltpu.roll(dq_fold, 64, 1)
    dq_fold = dq_fold + pltpu.roll(dq_fold, 32, 1)
    group = iota((512, 128), 1) // 32
    h0, h1, h2 = pieces(dq_fold)
    dq_split = jnp.where(group == 0, h0, jnp.where(group == 1, h1, jnp.where(group == 2, h2, 0.0))).astype(BF16)
    back = ones_where(jnp.logical_and(row_b // 8 == row_a % 64, row_b % 8 == row_a // 64))
    dq_head = dot(back, dq_split)
    dq_head = dq_head + pltpu.roll(dq_head, 64, 1)
    dq_head = dq_head + pltpu.roll(dq_head, 32, 1)
    dq_head = dq_head.reshape(16, 32, 128)
    group8 = iota((16, 8, 128), 2) // 32
    dense = dq_head[:, 0:8, :]
    for at in range(1, 4):
        dense = jnp.where(group8 == at, dq_head[:, at * 8:(at + 1) * 8, :], dense)
    dq_send[...] = dense

    def p1_copy(at):
        return pltpu.make_async_remote_copy(
            src_ref=dq_send.at[at], dst_ref=dq_recv.at[zpos], send_sem=p1_send.at[at],
            recv_sem=p1_recv.at[zpos], device_id=device(at % 2, core * 8 + at // 2, ypos), device_id_type=MESH,
        )

    def p1_arrival(at):
        return pltpu.make_async_remote_copy(
            src_ref=dq_send.at[0], dst_ref=dq_recv.at[at], send_sem=p1_send.at[0],
            recv_sem=p1_recv.at[at], device_id=device(home, at, ypos), device_id_type=MESH,
        )

    def p1_start(at, carry):
        @pl.when(jnp.logical_not(jnp.logical_and(at % 2 == core, core * 8 + at // 2 == zpos)))
        def _():
            p1_copy(at).start()

        return carry

    lax.fori_loop(0, 16, p1_start, 0)

    @pl.when(is_home)
    def _():
        dq_recv[zpos] = dq_send[slot * 2 + core]

    def p2_copy(step):
        return pltpu.make_async_remote_copy(
            src_ref=dq_recv, dst_ref=dq_peers.at[key], send_sem=p2_send.at[step],
            recv_sem=p2_recv.at[key], device_id=(core, (key + step) % 8, col), device_id_type=MESH,
        )

    def p2_arrival(step):
        peer = (key + step) % 8
        return pltpu.make_async_remote_copy(
            src_ref=dq_recv, dst_ref=dq_peers.at[peer], send_sem=p2_send.at[step],
            recv_sem=p2_recv.at[peer], device_id=(core, peer, col), device_id_type=MESH,
        )

    def phase_two():
        def p1_wait(at, carry):
            @pl.when(jnp.logical_not(jnp.logical_and(is_home, at == zpos)))
            def _():
                p1_arrival(at).wait_recv()

            return carry

        lax.fori_loop(0, 16, p1_wait, 0)
        dq_peers[key] = dq_recv[...]

        def p2_start(step, carry):
            p2_copy(step).start()
            return carry

        lax.fori_loop(1, 8, p2_start, 0)

    win = win_v[...]

    def gp_copy(pair):
        return pltpu.make_async_copy(gp_v.at[pl.ds(pair * 2, 2)], gp_hbm.at[pl.ds(pair * 2, 2)], gp_sem.at[pair])

    def backward_pair(pair):
        at = pl.ds(pl.multiple_of(pair * 16, 16), 16)
        dhidden = dot(w2_v[...], ds_in[:, at, :].reshape(64, 1024))
        for r in range(2):
            row = pair * 2 + r
            dpre = (dhidden[r * 256:(r + 1) * 256] * slope_v[row].astype(F32)).astype(BF16)
            dunit = dot(win, dpre) * gain_col
            inv_std = stat_v[row, 1:2, :]
            unit = (x_v[row].astype(F32) - stat_v[row, 0:1, :]) * inv_std
            first = jnp.sum(dunit, axis=0, keepdims=True) * (1.0 / 64.0)
            second = jnp.sum(dunit * unit, axis=0, keepdims=True) * (1.0 / 64.0)
            gp_v[row] = (inv_std * (dunit - first - unit * second)).astype(BF16)
        gp_copy(pair).start()

    def backward_body(pair, carry):
        @pl.when(pair % 2 == 0)
        def _():
            for step in (1, 2, 3):
                ds_arrival(step, pair // 2).wait_recv()

        backward_pair(pair)
        for at, (far, half) in ((1, (6, 1)), (2, (6, 0)), (4, (4, 1)), (6, (4, 0))):
            @pl.when(pair == at)
            def _():
                rs_sum(far, half)

        @pl.when(pair == 5)
        def _():
            phase_two()

        return carry

    lax.fori_loop(0, 8, backward_body, 0)
    rs_sum(2, 1)
    rs_sum(2, 0)

    sibling, _ = quad(2)

    def f_copy():
        return pltpu.make_async_remote_copy(
            src_ref=gkv_v, dst_ref=gkv_v, send_sem=f_send, recv_sem=f_recv,
            device_id=sibling, device_id_type=MESH,
        )

    @pl.when(is_home)
    def _():
        total = dkv_v[slot]
        for way, recv in ((0, rsp_recv), (1, rsm_recv)):
            for far in (1, 2):
                for half in range(2):
                    rs_copy(way, far, half).wait_recv()
                total = total + recv[far - 1].reshape(64, 1024).astype(F32)
        gkv_v[0:32, :] = (total[0:32] * score_scale).astype(BF16)
        gkv_v[32:64, :] = total[32:64].astype(BF16)
        f_copy().start()

    def p2_wait(step, carry):
        p2_arrival(step).wait_recv()
        return carry

    lax.fori_loop(1, 8, p2_wait, 0)
    total_q = dq_peers[0]
    for at in range(1, 8):
        total_q = total_q + dq_peers[at]
    final_q = (total_q.reshape(128, 128) * score_scale).astype(BF16).astype(F32).T.astype(BF16)
    lane_a, lane_b = iota((128, 512), 0), iota((128, 512), 1)
    grad_q = jnp.zeros((32, 512), F32)
    for at in range(4):
        place = jnp.logical_and(
            lane_a // 8 == lane_b // 32,
            jnp.logical_and(lane_a % 8 == lane_b % 8, (lane_b // 8) % 4 == at),
        )
        grad_q = grad_q + dot(final_q[at * 32:(at + 1) * 32, :], ones_where(place))
    gq_v[...] = grad_q.astype(BF16)
    gq_copy = pltpu.make_async_copy(gq_v, gq_hbm.at[0], o_sem.at[0])
    gq_copy.start()

    @pl.when(jnp.logical_not(is_home))
    def _():
        f_copy().wait_recv()

    gk_copy = pltpu.make_async_copy(gkv_v.at[pl.ds(0, 32)], gk_hbm.at[0], o_sem.at[1])
    gv_copy = pltpu.make_async_copy(gkv_v.at[pl.ds(32, 32)], gv_hbm.at[0], o_sem.at[2])
    gk_copy.start()
    gv_copy.start()

    @pl.when(is_home)
    def _():
        f_copy().wait_send()
        for half in range(2):
            for hops in (2, 1):
                ag_copy(half, slot, 0, hops).wait_send()
                ag_copy(half, slot, 1, hops).wait_send()

    for half in range(2):
        for hops in (2, 4, 6):
            ag_forward(half, hops, True)

    def z_drain(at, carry):
        @pl.when(jnp.logical_not(jnp.logical_and(is_home, at == zpos)))
        def _():
            q_copy(at).wait_send()

        @pl.when(jnp.logical_not(jnp.logical_and(at % 2 == core, core * 8 + at // 2 == zpos)))
        def _():
            p1_copy(at).wait_send()

        return carry

    lax.fori_loop(0, 16, z_drain, 0)
    for step in (1, 2, 3):
        bias_all(step).wait_send()
        for piece in range(4):
            ds_copy(step, piece).wait_send()

    for half in range(2):
        for way, last in ((0, 8), (1, 7)):
            for far in range(1, last + 1):
                @pl.when(rs_dest(way, far) // 8 == core)
                def _():
                    rs_copy(way, far, half).wait_send()

    def last_drain(step, carry):
        p2_copy(step).wait_send()
        return carry

    lax.fori_loop(1, 8, last_drain, 0)

    def gp_drain(pair, carry):
        gp_copy(pair).wait()
        return carry

    lax.fori_loop(0, 8, gp_drain, 0)
    gq_copy.wait()
    gk_copy.wait()
    gv_copy.wait()


def hand_over(gp_in, gq_in, gk_in, gv_in, gp_out, gq_out, gk_out, gv_out, row_sem, small_sem):
    copies = [pltpu.make_async_copy(gp_in.at[row], gp_out.at[row], row_sem.at[row]) for row in range(16)]
    for at, (src, dst) in enumerate(((gq_in, gq_out), (gk_in, gk_out), (gv_in, gv_out))):
        copies.append(pltpu.make_async_copy(src, dst, small_sem.at[at]))
    for copy in copies:
        copy.start()
    for copy in copies:
        copy.wait()


def per_device(
    pair_feats, bucket_ids, ln_gain, w_in, b_in, w_out, bucket_table, key_mask,
    q_heads, k_heads, v_heads, out_heads, dout_heads, log_norm,
):
    any_space = pl.BlockSpec(memory_space=pl.ANY)
    vmem = pltpu.VMEM
    dma = pltpu.SemaphoreType.DMA
    results = pl.pallas_call(
        kernel,
        out_shape=(
            jax.ShapeDtypeStruct((16, 64, 1024), BF16),
            jax.ShapeDtypeStruct((1, 32, 512), BF16),
            jax.ShapeDtypeStruct((1, 32, 1024), BF16),
            jax.ShapeDtypeStruct((1, 32, 1024), BF16),
        ),
        in_specs=[any_space] * 14,
        out_specs=(any_space,) * 4,
        scratch_shapes=[
            vmem((16, 64, 1024), BF16),
            vmem((16, 1024), jnp.int32),
            vmem((1, 64), F32),
            vmem((64, 256), BF16),
            vmem((1, 256), F32),
            vmem((32, 256), BF16),
            vmem((32, 32), BF16),
            vmem((1, 1024), jnp.int32),
            vmem((1, 32, 512), BF16),
            vmem((1, 32, 512), BF16),
            vmem((1, 32, 512), BF16),
            vmem((1, 512), F32),
            vmem((16, 64, 1024), BF16),
            vmem((32, 512), BF16),
            vmem((64, 1024), BF16),
            vmem((16, 256, 1024), BF16),
            vmem((16, 2, 1024), F32),
            vmem((2, 8, 32, 1024), BF16),
            vmem((4, 8, 16, 1024), BF16),
            vmem((4, 8, 16, 1024), BF16),
            vmem((4, 128, 1024), BF16),
            vmem((4, 128, 1024), BF16),
            vmem((512, 1024), BF16),
            vmem((512, 1024), F32),
            vmem((16, 32, 128), BF16),
            vmem((16, 32, 128), BF16),
            vmem((512, 256), BF16),
            vmem((512, 256), BF16),
            vmem((512, 128), F32),
            vmem((512, 128), F32),
            vmem((8, 64, 1024), F32),
            vmem((8, 2, 32, 1024), BF16),
            vmem((8, 2, 32, 1024), BF16),
            vmem((7, 2, 32, 1024), BF16),
            vmem((7, 2, 32, 1024), BF16),
            vmem((16, 8, 128), F32),
            vmem((16, 8, 128), F32),
            vmem((8, 16, 8, 128), F32),
            vmem((512, 128), BF16),
            vmem((512, 64), BF16),
            vmem((32, 256), BF16),
            vmem((32, 32), BF16),
            dma((11,)), dma((8,)), dma((2,)), dma((8,)), dma((3,)),
            dma((2, 4, 8)), dma((2, 8)), dma((16,)), dma((16,)), dma((4,)), dma((4,)), dma((4, 4)), dma((4, 4)),
            dma((8, 2)), dma((8, 2)), dma((7, 2)), dma((7, 2)), dma, dma,
            dma((16,)), dma((16,)), dma((8,)), dma((8,)),
            pltpu.SemaphoreType.REGULAR, pltpu.SemaphoreType.REGULAR,
        ],
        compiler_params=pltpu.CompilerParams(
            collective_id=0, has_side_effects=True, vmem_limit_bytes=56 * 2**20
        ),
        name="pair_attention_backward",
    )(
        pair_feats, bucket_ids, ln_gain.reshape(1, 64), w_in, b_in.reshape(1, 256), w_out.T,
        bucket_table, key_mask.reshape(1, 1024), q_heads, k_heads, v_heads, out_heads, dout_heads, log_norm,
    )
    return pl.pallas_call(
        hand_over,
        out_shape=tuple(jax.ShapeDtypeStruct(member.shape, member.dtype) for member in results),
        in_specs=[any_space] * 4,
        out_specs=(any_space,) * 4,
        scratch_shapes=[dma((16,)), dma((3,))],
        name="hand_over",
    )(*results)


def solution(mesh):
    return jax.shard_map(
        per_device,
        mesh=mesh,
        in_specs=(
            P(("query", "heads"), None, "key"),
            P(("query", "heads"), "key"),
            P(),
            P(),
            P(),
            P(),
            P(),
            P("key"),
            P("heads", None, "query"),
            P("heads", None, "key"),
            P("heads", None, "key"),
            P("heads", None, "query"),
            P("heads", None, "query"),
            P("heads", "query"),
        ),
        out_specs=(
            P(("query", "heads"), None, "key"),
            P("heads", None, "query"),
            P("heads", None, "key"),
            P("heads", None, "key"),
        ),
        check_vma=False,
    )
```

```python
import functools
import math

import jax
import jax.numpy as jnp
from jax import lax
from jax.experimental import pallas as pl
from jax.experimental.pallas import tpu as pltpu
from jax.sharding import PartitionSpec as P

F32 = jnp.float32
BF16 = jnp.bfloat16
MESH = pl.DeviceIdType.MESH


def dot(lhs, rhs):
    return jnp.dot(lhs, rhs, preferred_element_type=F32)


def iota(shape, axis):
    return lax.broadcasted_iota(jnp.int32, shape, axis)


def ones_where(cond):
    return jnp.where(cond, 1.0, 0.0).astype(BF16)


def column(row):
    size = row.shape[1]
    diag = iota((size, size), 0) == iota((size, size), 1)
    return jnp.sum(jnp.where(diag, jnp.broadcast_to(row, (size, size)), 0.0), axis=1, keepdims=True)


def pieces(value):
    first = value.astype(BF16).astype(F32)
    second = (value - first).astype(BF16).astype(F32)
    third = (value - first - second).astype(BF16).astype(F32)
    return first, second, third


def gelu_parts(pre_act):
    cdf_val = 0.5 * (1.0 + lax.erf(pre_act * (1.0 / math.sqrt(2.0))))
    density = jnp.exp(-0.5 * pre_act * pre_act) * (1.0 / math.sqrt(2.0 * math.pi))
    return pre_act * cdf_val, cdf_val + pre_act * density


def kernel(
    x_hbm, bucket_hbm, gain_hbm, win_hbm, bin_hbm, woutt_hbm, table_hbm, mask_hbm,
    q_hbm, k_hbm, v_hbm, out_hbm, dout_hbm, norm_hbm,
    gp_hbm, gq_hbm, gk_hbm, gv_hbm,
    x_v, bucket_v, gain_v, win_v, bin_v, woutt_v, table_v, mask_v,
    q_v, out_v, dout_v, norm_v,
    gp_v, gq_v, gkv_v,
    slope_v, stat_v, kv_v, bias_out, bias_in, ds_all, ds_in, probs_v, probs_f,
    qstage, qrecv, qblk_v, doblk_v, norm_b, delta_b, dkv_v,
    rsp_send, rsp_recv, rsm_send, rsm_recv,
    dq_send, dq_recv, dq_peers, w1_v, w2_v, wmix_v, tab_v,
    in_sem, x_sem, kv_sem, gp_sem, o_sem,
    ag_send, ag_recv, q_send, q_recv, b_send, b_recv, d_send, d_recv,
    rp_send, rp_recv, rm_send, rm_recv, f_send, f_recv,
    p1_send, p1_recv, p2_send, p2_recv, round_one, round_two,
):
    core = lax.axis_index("query")
    key = lax.axis_index("key")
    col = lax.axis_index("heads")
    zpos = col // 2
    ypos = col % 2
    home = zpos // 8
    slot = zpos % 8
    mine = core * 2 + ypos
    is_home = home == core
    score_scale = 1.0 / math.sqrt(32.0)

    def device(core_at, z_at, y_at):
        return (core_at, key, z_at * 2 + y_at)

    def along(hops):
        return device(core, (zpos + 16 + hops) % 16, ypos)

    def along_x(hops):
        return (core, (key + 8 + 2 * hops) % 8, col)

    across_y = (core, key + 1 - 2 * (key % 2), col)

    def quad(step):
        core_at = (core + step // 2) % 2
        y_at = (ypos + step % 2) % 2
        return device(core_at, zpos, y_at), core_at * 2 + y_at

    barrier = pltpu.get_barrier_semaphore()

    def greet(where):
        pl.semaphore_signal(barrier, inc=1, device_id=where, device_id_type=MESH)

    for hops in (1, -1, 2, -2):
        greet(along(hops))
        greet(device(1 - core, (zpos + 16 + hops) % 16, ypos))
    for step in (1, 2, 3):
        greet(quad(step)[0])
    greet(along_x(1))
    greet(along_x(-1))
    greet(across_y)

    loads = [
        pltpu.make_async_copy(src, dst, in_sem.at[at])
        for at, (src, dst) in enumerate(
            (
                (gain_hbm, gain_v), (win_hbm, win_v), (bin_hbm, bin_v), (woutt_hbm, woutt_v),
                (table_hbm, table_v), (bucket_hbm, bucket_v), (mask_hbm, mask_v), (q_hbm, q_v),
                (out_hbm, out_v), (dout_hbm, dout_v), (norm_hbm, norm_v),
            )
        )
    ]
    for load in loads:
        load.start()

    def x_load(pair):
        return pltpu.make_async_copy(x_hbm.at[pl.ds(pair * 2, 2)], x_v.at[pl.ds(pair * 2, 2)], x_sem.at[pair])

    for pair in range(8):
        x_load(pair).start()

    k_load = pltpu.make_async_copy(k_hbm.at[0], kv_v.at[0, slot], kv_sem.at[0])
    v_load = pltpu.make_async_copy(v_hbm.at[0], kv_v.at[1, slot], kv_sem.at[1])

    @pl.when(is_home)
    def _():
        k_load.start()
        v_load.start()

    for load in loads:
        load.wait()

    sel_row = iota((32, 32), 0)
    part_at, head_at = sel_row // 8, sel_row % 8
    head_of = 2 * (8 * (part_at // 2) + head_at) + part_at % 2
    select = ones_where(iota((32, 32), 1) == head_of)
    woutt = woutt_v[...]
    wmix_v[...] = dot(select, woutt).astype(BF16)
    tab_v[...] = dot(select, table_v[...].T).astype(BF16)
    row64 = iota((64, 32), 0)
    part64, head64 = row64 // 16, row64 % 8
    head_of64 = 2 * (8 * (part64 // 2) + head64) + part64 % 2
    spread = dot(ones_where(iota((64, 32), 1) == head_of64), woutt).T
    parity = (iota((256, 64), 1) // 8) % 2
    w2_v[0:256, :] = jnp.where(parity == 0, spread, 0.0).astype(BF16)
    w2_v[256:512, :] = jnp.where(parity == 1, spread, 0.0).astype(BF16)
    win_t = win_v[...].astype(F32).T
    zero = jnp.zeros((256, 64), F32)
    w1_v[0:256, :] = jnp.concatenate([win_t, zero], axis=1).astype(BF16)
    w1_v[256:512, :] = jnp.concatenate([zero, win_t], axis=1).astype(BF16)
    gain_col = column(gain_v[...])
    bin_col = column(bin_v[...])

    dout_f = dout_v[0].astype(F32)
    delta = jnp.sum(dout_f * out_v[0].astype(F32), axis=0, keepdims=True)
    n0, n1, n2 = pieces(norm_v[...])
    d0, d1, d2 = pieces(delta)
    sub = iota((64, 512), 0)
    extra = jnp.zeros((64, 512), F32)
    for at, piece in enumerate((n0, n1, n2, d0, d1, d2)):
        extra = jnp.where(sub == at, jnp.broadcast_to(piece, (64, 512)), extra)
    packed = jnp.concatenate([q_v[0].astype(F32), dout_f, extra], axis=0)
    qstage[...] = packed.T.astype(BF16).reshape(16, 32, 128)

    def q_copy(at):
        return pltpu.make_async_remote_copy(
            src_ref=qstage.at[at], dst_ref=qrecv.at[slot * 2 + core], send_sem=q_send.at[at],
            recv_sem=q_recv.at[slot * 2 + core], device_id=device(home, at, ypos), device_id_type=MESH,
        )

    def q_arrival(at):
        return pltpu.make_async_remote_copy(
            src_ref=qstage.at[0], dst_ref=qrecv.at[at], send_sem=q_send.at[0],
            recv_sem=q_recv.at[at], device_id=device(at % 2, core * 8 + at // 2, ypos), device_id_type=MESH,
        )

    def ag_copy(half, at, way, hops):
        return pltpu.make_async_remote_copy(
            src_ref=kv_v.at[half, at], dst_ref=kv_v.at[half, at],
            send_sem=ag_send.at[half, way * 2 + hops - 1, at],
            recv_sem=ag_recv.at[half, at], device_id=along(hops - 2 * hops * way), device_id_type=MESH,
        )

    def ag_source(way, hops):
        return (zpos + 16 - hops + 2 * hops * way) % 16

    def ag_forward(half, hops, ending=False):
        for way in range(2):
            source = ag_source(way, hops)

            @pl.when(source // 8 == core)
            def _():
                onward = [ag_copy(half, source % 8, way, hop) for hop in ((1,) if way == 1 and hops == 6 else (2, 1))]
                if ending:
                    for copy in onward:
                        copy.wait_send()
                else:
                    onward[0].wait_recv()
                    for copy in onward:
                        copy.start()

    def ag_finish(half):
        for way, hops in ((0, 1), (0, 3), (0, 5), (0, 7), (0, 8), (1, 1), (1, 3), (1, 5), (1, 7)):
            source = ag_source(way, hops)

            @pl.when(source // 8 == core)
            def _():
                ag_copy(half, source % 8, way, 1).wait_recv()

    def bias_copy(step, pair):
        where, part = quad(step)
        return pltpu.make_async_remote_copy(
            src_ref=bias_out.at[part, pair], dst_ref=bias_in.at[mine, pair], send_sem=b_send.at[step],
            recv_sem=b_recv.at[mine], device_id=where, device_id_type=MESH,
        )

    def bias_all(step):
        where, part = quad(step)
        return pltpu.make_async_remote_copy(
            src_ref=bias_out.at[part], dst_ref=bias_in.at[part], send_sem=b_send.at[step],
            recv_sem=b_recv.at[part], device_id=where, device_id_type=MESH,
        )

    def forward_pair(pair):
        x_load(pair).wait()
        mats = []
        for r in range(2):
            values = x_v[pair * 2 + r].astype(F32)
            mean = jnp.sum(values, axis=0, keepdims=True) * (1.0 / 64.0)
            centre = values - mean
            inv_std = lax.rsqrt(jnp.sum(centre * centre, axis=0, keepdims=True) * (1.0 / 64.0) + 1e-05)
            stat_v[pair * 2 + r, 0:1, :] = mean
            stat_v[pair * 2 + r, 1:2, :] = inv_std
            mats.append((centre * inv_std * gain_col).astype(BF16))
        pre = dot(w1_v[...], jnp.concatenate(mats, axis=0))
        mixes = []
        for r in range(2):
            gelu_val, gelu_slope = gelu_parts(pre[r * 256:(r + 1) * 256] + bin_col)
            slope_v[pair * 2 + r] = gelu_slope.astype(BF16)
            hidden = gelu_val.astype(BF16)
            onehot = ones_where(bucket_v[pl.ds(pair * 2 + r, 1), :] == iota((32, 1024), 0))
            mixes.append(dot(wmix_v[...], hidden) + dot(tab_v[...], onehot))
        for part in range(4):
            rows = [mix[part * 8:(part + 1) * 8] for mix in mixes]
            bias_out[part, pair] = jnp.concatenate(rows, axis=0).astype(BF16)

    def bias_send(pair):
        for step in (1, 2, 3):
            bias_copy(step, pair).start()

    pl.semaphore_wait(barrier, 14)

    @pl.when(is_home)
    def _():
        k_load.wait()
        v_load.wait()
        for half in range(2):
            for hops in (2, 1):
                ag_copy(half, slot, 0, hops).start()
                ag_copy(half, slot, 1, hops).start()

    for where in (along(2), along(-2), along_x(1), along_x(-1)):
        pl.semaphore_signal(round_one, inc=1, device_id=where, device_id_type=MESH)

    def q_start(at, carry):
        @pl.when(jnp.logical_not(jnp.logical_and(is_home, at == zpos)))
        def _():
            q_copy(at).start()

        return carry

    def forward_body(pair, carry):
        forward_pair(pair)
        bias_send(pair)

        @pl.when(pair == 2)
        def _():
            pl.semaphore_wait(round_one, 4)
            for where in (along(4), along(-4), across_y):
                pl.semaphore_signal(round_two, inc=1, device_id=where, device_id_type=MESH)
            ag_forward(0, 2)

        @pl.when(pair == 3)
        def _():
            ag_forward(1, 2)

        @pl.when(pair == 5)
        def _():
            ag_forward(0, 4)
            pl.semaphore_wait(round_two, 3)
            lax.fori_loop(0, 16, q_start, 0)

        @pl.when(pair == 6)
        def _():
            ag_forward(1, 4)

        return carry

    lax.fori_loop(0, 8, forward_body, 0)

    @pl.when(is_home)
    def _():
        qrecv[slot * 2 + core] = qstage[zpos]

    ag_forward(0, 6)

    def q_wait(at, carry):
        @pl.when(jnp.logical_not(jnp.logical_and(at % 2 == core, core * 8 + at // 2 == zpos)))
        def _():
            q_arrival(at).wait_recv()

        return carry

    lax.fori_loop(0, 16, q_wait, 0)
    arrived = qrecv[...].reshape(512, 128)
    row_a, row_b = iota((512, 512), 0), iota((512, 512), 1)
    order = ones_where(jnp.logical_and(row_a // 8 == row_b % 64, row_a % 8 == row_b // 64))
    by_row = dot(order, arrived).astype(BF16)
    lane, spot = iota((128, 256), 0), iota((128, 256), 1)
    own_head = iota((512, 256), 0) % 8 == iota((512, 256), 1) // 32
    qblk_v[...] = jnp.where(own_head, dot(by_row, ones_where(lane == spot % 32)), 0.0).astype(BF16)
    doblk_v[...] = jnp.where(own_head, dot(by_row, ones_where(lane == 32 + spot % 32)), 0.0).astype(BF16)
    wide = iota((128, 128), 0)
    norm_b[...] = dot(by_row, ones_where(jnp.logical_and(wide >= 64, wide < 67)))
    delta_b[...] = dot(by_row, ones_where(jnp.logical_and(wide >= 67, wide < 70)))

    ag_forward(1, 6)
    live = mask_v[...] == 1
    ag_finish(0)
    keys = kv_v[0].reshape(256, 1024)

    for step in (1, 2, 3, 0):
        _, part = quad(step)
        if step:
            bias_all(step).wait_recv()
            bias = bias_in[part]
        else:
            bias = bias_out[part]
        rows = pl.ds(pl.multiple_of(part * 128, 128), 128)
        scores = dot(qblk_v[rows, :], keys) * score_scale + bias.reshape(128, 1024).astype(F32)
        shift = jnp.concatenate([norm_b[rows, :]] * 8, axis=1)
        probs = jnp.where(live, jnp.exp(scores - shift), 0.0)
        probs_f[rows, :] = probs
        probs_v[rows, :] = probs.astype(BF16)
    dkv_v[:, 32:64, :] = dot(doblk_v[...].T, probs_v[...]).reshape(8, 32, 1024)

    def rs_copy(way, far, half):
        hops = 2 if far == 8 or far % 2 == 0 else 1
        send, recv, s_sem, r_sem = (
            (rsp_send, rsp_recv, rp_send, rp_recv), (rsm_send, rsm_recv, rm_send, rm_recv)
        )[way]
        return pltpu.make_async_remote_copy(
            src_ref=send.at[far - 1, half], dst_ref=recv.at[far - 1, half], send_sem=s_sem.at[far - 1, half],
            recv_sem=r_sem.at[far - 1, half], device_id=along(-hops if way else hops), device_id_type=MESH,
        )

    def rs_dest(way, far):
        return (zpos + 16 - far if way else zpos + far) % 16

    def rs_part(far, half, way):
        dest = rs_dest(way, far)
        send, recv = ((rsp_send, rsp_recv), (rsm_send, rsm_recv))[way]
        last = 7 if way else 8

        @pl.when(dest // 8 == core)
        def _():
            total = dkv_v[dest % 8, half * 32:half * 32 + 32, :]
            if far in (2, 4, 6):
                for other in (far + 1, far + 2):
                    if other <= last:
                        rs_copy(way, other, half).wait_recv()
                        total = total + recv[other - 1, half].astype(F32)
            send[far - 1, half] = total.astype(BF16)
            rs_copy(way, far, half).start()

    def rs_raw(half):
        for far in (8, 7, 5, 3, 1):
            for way in range(2):
                if not (way == 1 and far == 8):
                    rs_part(far, half, way)

    def rs_sum(far, half):
        for way in range(2):
            rs_part(far, half, way)

    rs_raw(1)
    ag_finish(1)
    values = kv_v[1].reshape(256, 1024)

    def ds_copy(step, piece):
        where, part = quad(step)
        at = pl.ds(piece * 32, 32)
        return pltpu.make_async_remote_copy(
            src_ref=ds_all.at[part, at], dst_ref=ds_in.at[mine, at], send_sem=d_send.at[step, piece],
            recv_sem=d_recv.at[mine, piece], device_id=where, device_id_type=MESH,
        )

    def ds_arrival(step, piece):
        where, part = quad(step)
        at = pl.ds(pl.multiple_of(piece * 32, 32), 32)
        return pltpu.make_async_remote_copy(
            src_ref=ds_all.at[part, at], dst_ref=ds_in.at[part, at], send_sem=d_send.at[step, piece],
            recv_sem=d_recv.at[part, piece], device_id=where, device_id_type=MESH,
        )

    for step in (1, 3, 2, 0):
        _, part = quad(step)
        rows = pl.ds(pl.multiple_of(part * 128, 128), 128)
        less = jnp.concatenate([delta_b[rows, :]] * 8, axis=1)
        dscores = (probs_f[rows, :] * (dot(doblk_v[rows, :], values) - less)).astype(BF16)
        ds_all[part] = dscores
        if not step:
            ds_in[part] = dscores
    for piece in range(4):
        for step in (1, 3, 2):
            ds_copy(step, piece).start()
    ds_flat = ds_all[...].reshape(512, 1024)
    dq_full = lax.dot_general(ds_flat, keys, (((1,), (1,)), ((), ())), preferred_element_type=F32)
    dq_full = jnp.where(own_head, dq_full, 0.0)
    dq_fold = dq_full[:, 0:128] + dq_full[:, 128:256]
    dq_fold = dq_fold + pltpu.roll(dq_fold, 64, 1)
    dq_fold = dq_fold + pltpu.roll(dq_fold, 32, 1)
    group = iota((512, 128), 1) // 32
    h0, h1, h2 = pieces(dq_fold)
    dq_split = jnp.where(group == 0, h0, jnp.where(group == 1, h1, jnp.where(group == 2, h2, 0.0))).astype(BF16)
    back = ones_where(jnp.logical_and(row_b // 8 == row_a % 64, row_b % 8 == row_a // 64))
    dq_head = dot(back, dq_split)
    dq_head = dq_head + pltpu.roll(dq_head, 64, 1)
    dq_head = dq_head + pltpu.roll(dq_head, 32, 1)
    dq_head = dq_head.reshape(16, 32, 128)
    group8 = iota((16, 8, 128), 2) // 32
    dense = dq_head[:, 0:8, :]
    for at in range(1, 4):
        dense = jnp.where(group8 == at, dq_head[:, at * 8:(at + 1) * 8, :], dense)
    dq_send[...] = dense

    def p1_copy(at):
        return pltpu.make_async_remote_copy(
            src_ref=dq_send.at[at], dst_ref=dq_recv.at[zpos], send_sem=p1_send.at[at],
            recv_sem=p1_recv.at[zpos], device_id=device(at % 2, core * 8 + at // 2, ypos), device_id_type=MESH,
        )

    def p1_arrival(at):
        return pltpu.make_async_remote_copy(
            src_ref=dq_send.at[0], dst_ref=dq_recv.at[at], send_sem=p1_send.at[0],
            recv_sem=p1_recv.at[at], device_id=device(home, at, ypos), device_id_type=MESH,
        )

    def p1_start(at, carry):
        @pl.when(jnp.logical_not(jnp.logical_and(at % 2 == core, core * 8 + at // 2 == zpos)))
        def _():
            p1_copy(at).start()

        return carry

    lax.fori_loop(0, 16, p1_start, 0)

    @pl.when(is_home)
    def _():
        dq_recv[zpos] = dq_send[slot * 2 + core]

    dkv_v[:, 0:32, :] = dot(qblk_v[...].T, ds_flat).reshape(8, 32, 1024)
    rs_raw(0)
    rs_sum(6, 1)

    def p2_copy(step):
        return pltpu.make_async_remote_copy(
            src_ref=dq_peers.at[key], dst_ref=dq_peers.at[key], send_sem=p2_send.at[step],
            recv_sem=p2_recv.at[key], device_id=(core, (key + step) % 8, col), device_id_type=MESH,
        )

    def p2_arrival(step):
        peer = (key + step) % 8
        return pltpu.make_async_remote_copy(
            src_ref=dq_peers.at[key], dst_ref=dq_peers.at[peer], send_sem=p2_send.at[step],
            recv_sem=p2_recv.at[peer], device_id=(core, peer, col), device_id_type=MESH,
        )

    def phase_two():
        def p1_wait(at, carry):
            @pl.when(jnp.logical_not(jnp.logical_and(is_home, at == zpos)))
            def _():
                p1_arrival(at).wait_recv()

            return carry

        lax.fori_loop(0, 16, p1_wait, 0)
        dq_peers[key] = dq_recv[...].reshape(128, 128).astype(BF16)

        def p2_start(step, carry):
            p2_copy(step).start()
            return carry

        lax.fori_loop(1, 8, p2_start, 0)

    win = win_v[...]

    def gp_copy(pair):
        return pltpu.make_async_copy(gp_v.at[pl.ds(pair * 2, 2)], gp_hbm.at[pl.ds(pair * 2, 2)], gp_sem.at[pair])

    def backward_pair(pair):
        at = pl.ds(pl.multiple_of(pair * 16, 16), 16)
        dhidden = dot(w2_v[...], ds_in[:, at, :].reshape(64, 1024))
        for r in range(2):
            row = pair * 2 + r
            dpre = (dhidden[r * 256:(r + 1) * 256] * slope_v[row].astype(F32)).astype(BF16)
            dunit = dot(win, dpre) * gain_col
            inv_std = stat_v[row, 1:2, :]
            unit = (x_v[row].astype(F32) - stat_v[row, 0:1, :]) * inv_std
            first = jnp.sum(dunit, axis=0, keepdims=True) * (1.0 / 64.0)
            second = jnp.sum(dunit * unit, axis=0, keepdims=True) * (1.0 / 64.0)
            gp_v[row] = (inv_std * (dunit - first - unit * second)).astype(BF16)
        gp_copy(pair).start()

    def backward_body(pair, carry):
        @pl.when(pair % 2 == 0)
        def _():
            for step in (1, 2, 3):
                ds_arrival(step, pair // 2).wait_recv()

        backward_pair(pair)
        for at, (far, half) in ((1, (6, 0)), (2, (4, 1)), (4, (4, 0)), (6, (2, 1))):
            @pl.when(pair == at)
            def _():
                rs_sum(far, half)

        @pl.when(pair == 5)
        def _():
            phase_two()

        return carry

    lax.fori_loop(0, 8, backward_body, 0)
    rs_sum(2, 0)

    sibling, _ = quad(2)

    def f_copy():
        return pltpu.make_async_remote_copy(
            src_ref=gkv_v, dst_ref=gkv_v, send_sem=f_send, recv_sem=f_recv,
            device_id=sibling, device_id_type=MESH,
        )

    @pl.when(is_home)
    def _():
        total = dkv_v[slot]
        for way, recv in ((0, rsp_recv), (1, rsm_recv)):
            for far in (1, 2):
                for half in range(2):
                    rs_copy(way, far, half).wait_recv()
                total = total + recv[far - 1].reshape(64, 1024).astype(F32)
        gkv_v[0:32, :] = (total[0:32] * score_scale).astype(BF16)
        gkv_v[32:64, :] = total[32:64].astype(BF16)
        f_copy().start()

    def p2_wait(step, carry):
        p2_arrival(step).wait_recv()
        return carry

    lax.fori_loop(1, 8, p2_wait, 0)
    total_q = dq_peers[0].astype(F32)
    for at in range(1, 8):
        total_q = total_q + dq_peers[at].astype(F32)
    final_q = (total_q * score_scale).astype(BF16).astype(F32).T.astype(BF16)
    lane_a, lane_b = iota((128, 512), 0), iota((128, 512), 1)
    grad_q = jnp.zeros((32, 512), F32)
    for at in range(4):
        place = jnp.logical_and(
            lane_a // 8 == lane_b // 32,
            jnp.logical_and(lane_a % 8 == lane_b % 8, (lane_b // 8) % 4 == at),
        )
        grad_q = grad_q + dot(final_q[at * 32:(at + 1) * 32, :], ones_where(place))
    gq_v[...] = grad_q.astype(BF16)
    gq_copy = pltpu.make_async_copy(gq_v, gq_hbm.at[0], o_sem.at[0])
    gq_copy.start()

    @pl.when(jnp.logical_not(is_home))
    def _():
        f_copy().wait_recv()

    gk_copy = pltpu.make_async_copy(gkv_v.at[pl.ds(0, 32)], gk_hbm.at[0], o_sem.at[1])
    gv_copy = pltpu.make_async_copy(gkv_v.at[pl.ds(32, 32)], gv_hbm.at[0], o_sem.at[2])
    gk_copy.start()
    gv_copy.start()

    @pl.when(is_home)
    def _():
        f_copy().wait_send()
        for half in range(2):
            for hops in (2, 1):
                ag_copy(half, slot, 0, hops).wait_send()
                ag_copy(half, slot, 1, hops).wait_send()

    for half in range(2):
        for hops in (2, 4, 6):
            ag_forward(half, hops, True)

    def z_drain(at, carry):
        @pl.when(jnp.logical_not(jnp.logical_and(is_home, at == zpos)))
        def _():
            q_copy(at).wait_send()

        @pl.when(jnp.logical_not(jnp.logical_and(at % 2 == core, core * 8 + at // 2 == zpos)))
        def _():
            p1_copy(at).wait_send()

        return carry

    lax.fori_loop(0, 16, z_drain, 0)
    for step in (1, 2, 3):
        bias_all(step).wait_send()
        for piece in range(4):
            ds_copy(step, piece).wait_send()

    for half in range(2):
        for way, last in ((0, 8), (1, 7)):
            for far in range(1, last + 1):
                @pl.when(rs_dest(way, far) // 8 == core)
                def _():
                    rs_copy(way, far, half).wait_send()

    def last_drain(step, carry):
        p2_copy(step).wait_send()
        return carry

    lax.fori_loop(1, 8, last_drain, 0)

    def gp_drain(pair, carry):
        gp_copy(pair).wait()
        return carry

    lax.fori_loop(0, 8, gp_drain, 0)
    gq_copy.wait()
    gk_copy.wait()
    gv_copy.wait()


def hand_over(gp_in, gq_in, gk_in, gv_in, gp_out, gq_out, gk_out, gv_out, gp_v, gq_v, gk_v, gv_v, in_sem, out_sem):
    stages = [(gq_in, gq_v, gq_out), (gk_in, gk_v, gk_out), (gv_in, gv_v, gv_out)]
    for at in range(8):
        rows = pl.ds(at * 2, 2)
        stages.append((gp_in.at[rows], gp_v.at[rows], gp_out.at[rows]))
    loads = [pltpu.make_async_copy(src, mid, in_sem.at[at]) for at, (src, mid, _) in enumerate(stages)]
    stores = [pltpu.make_async_copy(mid, dst, out_sem.at[at]) for at, (_, mid, dst) in enumerate(stages)]
    for load in loads:
        load.start()
    for load, store in zip(loads, stores):
        load.wait()
        store.start()
    for store in stores:
        store.wait()


def per_device(
    pair_feats, bucket_ids, ln_gain, w_in, b_in, w_out, bucket_table, key_mask,
    q_heads, k_heads, v_heads, out_heads, dout_heads, log_norm,
):
    any_space = pl.BlockSpec(memory_space=pl.ANY)
    vmem = pltpu.VMEM
    dma = pltpu.SemaphoreType.DMA
    results = pl.pallas_call(
        kernel,
        out_shape=(
            jax.ShapeDtypeStruct((16, 64, 1024), BF16),
            jax.ShapeDtypeStruct((1, 32, 512), BF16),
            jax.ShapeDtypeStruct((1, 32, 1024), BF16),
            jax.ShapeDtypeStruct((1, 32, 1024), BF16),
        ),
        in_specs=[any_space] * 14,
        out_specs=(any_space,) * 4,
        scratch_shapes=[
            vmem((16, 64, 1024), BF16),
            vmem((16, 1024), jnp.int32),
            vmem((1, 64), F32),
            vmem((64, 256), BF16),
            vmem((1, 256), F32),
            vmem((32, 256), BF16),
            vmem((32, 32), BF16),
            vmem((1, 1024), jnp.int32),
            vmem((1, 32, 512), BF16),
            vmem((1, 32, 512), BF16),
            vmem((1, 32, 512), BF16),
            vmem((1, 512), F32),
            vmem((16, 64, 1024), BF16),
            vmem((32, 512), BF16),
            vmem((64, 1024), BF16),
            vmem((16, 256, 1024), BF16),
            vmem((16, 2, 1024), F32),
            vmem((2, 8, 32, 1024), BF16),
            vmem((4, 8, 16, 1024), BF16),
            vmem((4, 8, 16, 1024), BF16),
            vmem((4, 128, 1024), BF16),
            vmem((4, 128, 1024), BF16),
            vmem((512, 1024), BF16),
            vmem((512, 1024), F32),
            vmem((16, 32, 128), BF16),
            vmem((16, 32, 128), BF16),
            vmem((512, 256), BF16),
            vmem((512, 256), BF16),
            vmem((512, 128), F32),
            vmem((512, 128), F32),
            vmem((8, 64, 1024), F32),
            vmem((8, 2, 32, 1024), BF16),
            vmem((8, 2, 32, 1024), BF16),
            vmem((7, 2, 32, 1024), BF16),
            vmem((7, 2, 32, 1024), BF16),
            vmem((16, 8, 128), F32),
            vmem((16, 8, 128), F32),
            vmem((8, 128, 128), BF16),
            vmem((512, 128), BF16),
            vmem((512, 64), BF16),
            vmem((32, 256), BF16),
            vmem((32, 32), BF16),
            dma((11,)), dma((8,)), dma((2,)), dma((8,)), dma((3,)),
            dma((2, 4, 8)), dma((2, 8)), dma((16,)), dma((16,)), dma((4,)), dma((4,)), dma((4, 4)), dma((4, 4)),
            dma((8, 2)), dma((8, 2)), dma((7, 2)), dma((7, 2)), dma, dma,
            dma((16,)), dma((16,)), dma((8,)), dma((8,)),
            pltpu.SemaphoreType.REGULAR, pltpu.SemaphoreType.REGULAR,
        ],
        compiler_params=pltpu.CompilerParams(
            collective_id=0, has_side_effects=True, vmem_limit_bytes=56 * 2**20
        ),
        name="pair_attention_backward",
    )(
        pair_feats, bucket_ids, ln_gain.reshape(1, 64), w_in, b_in.reshape(1, 256), w_out.T,
        bucket_table, key_mask.reshape(1, 1024), q_heads, k_heads, v_heads, out_heads, dout_heads, log_norm,
    )
    return pl.pallas_call(
        hand_over,
        out_shape=tuple(jax.ShapeDtypeStruct(member.shape, member.dtype) for member in results),
        in_specs=[any_space] * 4,
        out_specs=(any_space,) * 4,
        scratch_shapes=[
            vmem((16, 64, 1024), BF16), vmem((1, 32, 512), BF16), vmem((1, 32, 1024), BF16), vmem((1, 32, 1024), BF16),
            dma((11,)), dma((11,)),
        ],
        name="hand_over",
    )(*results)


def solution(mesh):
    return jax.shard_map(
        per_device,
        mesh=mesh,
        in_specs=(
            P(("query", "heads"), None, "key"),
            P(("query", "heads"), "key"),
            P(),
            P(),
            P(),
            P(),
            P(),
            P("key"),
            P("heads", None, "query"),
            P("heads", None, "key"),
            P("heads", None, "key"),
            P("heads", None, "query"),
            P("heads", None, "query"),
            P("heads", "query"),
        ),
        out_specs=(
            P(("query", "heads"), None, "key"),
            P("heads", None, "query"),
            P("heads", None, "key"),
            P("heads", None, "key"),
        ),
        check_vma=False,
    )
```

```python
import functools
import math

import jax
import jax.numpy as jnp
from jax import lax
from jax.experimental import pallas as pl
from jax.experimental.pallas import tpu as pltpu
from jax.sharding import PartitionSpec as P

F32 = jnp.float32
BF16 = jnp.bfloat16
MESH = pl.DeviceIdType.MESH


def dot(lhs, rhs):
    return jnp.dot(lhs, rhs, preferred_element_type=F32)


def iota(shape, axis):
    return lax.broadcasted_iota(jnp.int32, shape, axis)


def ones_where(cond):
    return jnp.where(cond, 1.0, 0.0).astype(BF16)


def column(row):
    size = row.shape[1]
    diag = iota((size, size), 0) == iota((size, size), 1)
    return jnp.sum(jnp.where(diag, jnp.broadcast_to(row, (size, size)), 0.0), axis=1, keepdims=True)


def pieces(value):
    first = value.astype(BF16).astype(F32)
    second = (value - first).astype(BF16).astype(F32)
    third = (value - first - second).astype(BF16).astype(F32)
    return first, second, third


def gelu_parts(pre_act):
    cdf_val = 0.5 * (1.0 + lax.erf(pre_act * (1.0 / math.sqrt(2.0))))
    density = jnp.exp(-0.5 * pre_act * pre_act) * (1.0 / math.sqrt(2.0 * math.pi))
    return pre_act * cdf_val, cdf_val + pre_act * density


def kernel(
    x_hbm, bucket_hbm, gain_hbm, win_hbm, bin_hbm, woutt_hbm, table_hbm, mask_hbm,
    q_hbm, k_hbm, v_hbm, out_hbm, dout_hbm, norm_hbm,
    gp_hbm, gq_hbm, gk_hbm, gv_hbm,
    x_v, bucket_v, gain_v, win_v, bin_v, woutt_v, table_v, mask_v,
    q_v, out_v, dout_v, norm_v,
    gp_v, gq_v, gkv_v,
    slope_v, stat_v, kv_v, bias_out, bias_in, ds_all, ds_in, probs_v, probs_f,
    qstage, qrecv, qblk_v, doblk_v, qt_v, dot_v, norm_b, delta_b, dkv_v,
    rsp_send, rsp_recv, rsm_send, rsm_recv,
    dq_send, dq_recv, dq_peers, w1_v, w2_v, wmix_v, tab_v,
    in_sem, x_sem, kv_sem, gp_sem, o_sem,
    ag_send, ag_recv, q_send, q_recv, b_send, b_recv, d_send, d_recv,
    rp_send, rp_recv, rm_send, rm_recv, f_send, f_recv,
    p1_send, p1_recv, p2_send, p2_recv, round_one, round_two,
):
    core = lax.axis_index("query")
    key = lax.axis_index("key")
    col = lax.axis_index("heads")
    zpos = col // 2
    ypos = col % 2
    home = zpos // 8
    slot = zpos % 8
    mine = core * 2 + ypos
    is_home = home == core
    score_scale = 1.0 / math.sqrt(32.0)

    def device(core_at, z_at, y_at):
        return (core_at, key, z_at * 2 + y_at)

    def along(hops):
        return device(core, (zpos + 16 + hops) % 16, ypos)

    def along_x(hops):
        return (core, (key + 8 + 2 * hops) % 8, col)

    across_y = (core, key + 1 - 2 * (key % 2), col)

    def quad(step):
        core_at = (core + step // 2) % 2
        y_at = (ypos + step % 2) % 2
        return device(core_at, zpos, y_at), core_at * 2 + y_at

    barrier = pltpu.get_barrier_semaphore()

    def greet(where):
        pl.semaphore_signal(barrier, inc=1, device_id=where, device_id_type=MESH)

    for hops in (1, -1, 2, -2):
        greet(along(hops))
        greet(device(1 - core, (zpos + 16 + hops) % 16, ypos))
    for step in (1, 2, 3):
        greet(quad(step)[0])
    greet(along_x(1))
    greet(along_x(-1))
    greet(across_y)

    loads = [
        pltpu.make_async_copy(src, dst, in_sem.at[at])
        for at, (src, dst) in enumerate(
            (
                (gain_hbm, gain_v), (win_hbm, win_v), (bin_hbm, bin_v), (woutt_hbm, woutt_v),
                (table_hbm, table_v), (bucket_hbm, bucket_v), (mask_hbm, mask_v), (q_hbm, q_v),
                (out_hbm, out_v), (dout_hbm, dout_v), (norm_hbm, norm_v),
            )
        )
    ]
    for load in loads:
        load.start()

    def x_load(pair):
        return pltpu.make_async_copy(x_hbm.at[pl.ds(pair * 2, 2)], x_v.at[pl.ds(pair * 2, 2)], x_sem.at[pair])

    for pair in range(8):
        x_load(pair).start()

    k_load = pltpu.make_async_copy(k_hbm.at[0], kv_v.at[0, slot], kv_sem.at[0])
    v_load = pltpu.make_async_copy(v_hbm.at[0], kv_v.at[1, slot], kv_sem.at[1])

    @pl.when(is_home)
    def _():
        k_load.start()
        v_load.start()

    for load in loads:
        load.wait()

    sel_row = iota((32, 32), 0)
    part_at, head_at = sel_row // 8, sel_row % 8
    head_of = 2 * (8 * (part_at // 2) + head_at) + part_at % 2
    select = ones_where(iota((32, 32), 1) == head_of)
    woutt = woutt_v[...]
    wmix_v[...] = dot(select, woutt).astype(BF16)
    tab_v[...] = dot(select, table_v[...].T).astype(BF16)
    row64 = iota((64, 32), 0)
    part64, head64 = row64 // 16, row64 % 8
    head_of64 = 2 * (8 * (part64 // 2) + head64) + part64 % 2
    spread = dot(ones_where(iota((64, 32), 1) == head_of64), woutt).T
    parity = (iota((256, 64), 1) // 8) % 2
    w2_v[0:256, :] = jnp.where(parity == 0, spread, 0.0).astype(BF16)
    w2_v[256:512, :] = jnp.where(parity == 1, spread, 0.0).astype(BF16)
    win_t = win_v[...].astype(F32).T
    zero = jnp.zeros((256, 64), F32)
    w1_v[0:256, :] = jnp.concatenate([win_t, zero], axis=1).astype(BF16)
    w1_v[256:512, :] = jnp.concatenate([zero, win_t], axis=1).astype(BF16)
    gain_col = column(gain_v[...])
    bin_col = column(bin_v[...])

    dout_f = dout_v[0].astype(F32)
    delta = jnp.sum(dout_f * out_v[0].astype(F32), axis=0, keepdims=True)
    n0, n1, n2 = pieces(norm_v[...])
    d0, d1, d2 = pieces(delta)
    sub = iota((64, 512), 0)
    extra = jnp.zeros((64, 512), F32)
    for at, piece in enumerate((n0, n1, n2, d0, d1, d2)):
        extra = jnp.where(sub == at, jnp.broadcast_to(piece, (64, 512)), extra)
    packed = jnp.concatenate([q_v[0].astype(F32), dout_f, extra], axis=0)
    qstage[...] = packed.T.astype(BF16).reshape(16, 32, 128)

    def q_copy(at):
        return pltpu.make_async_remote_copy(
            src_ref=qstage.at[at], dst_ref=qrecv.at[slot * 2 + core], send_sem=q_send.at[at],
            recv_sem=q_recv.at[slot * 2 + core], device_id=device(home, at, ypos), device_id_type=MESH,
        )

    def q_arrival(at):
        return pltpu.make_async_remote_copy(
            src_ref=qstage.at[0], dst_ref=qrecv.at[at], send_sem=q_send.at[0],
            recv_sem=q_recv.at[at], device_id=device(at % 2, core * 8 + at // 2, ypos), device_id_type=MESH,
        )

    def ag_copy(half, at, way, hops):
        return pltpu.make_async_remote_copy(
            src_ref=kv_v.at[half, at], dst_ref=kv_v.at[half, at],
            send_sem=ag_send.at[half, way * 2 + hops - 1, at],
            recv_sem=ag_recv.at[half, at], device_id=along(hops - 2 * hops * way), device_id_type=MESH,
        )

    def ag_source(way, hops):
        return (zpos + 16 - hops + 2 * hops * way) % 16

    def ag_forward(half, hops, ending=False):
        for way in range(2):
            source = ag_source(way, hops)

            @pl.when(source // 8 == core)
            def _():
                two, one = (ag_copy(half, source % 8, way, hop) for hop in (2, 1))
                needed = source % 2 == way if hops == 6 else source >= 0
                if ending:
                    one.wait_send()

                    @pl.when(needed)
                    def _():
                        two.wait_send()
                else:
                    one.wait_recv()

                    @pl.when(needed)
                    def _():
                        two.start()

                    one.start()

    def ag_finish(half):
        for way, hops in ((0, 1), (0, 3), (0, 5), (0, 7), (0, 8), (1, 1), (1, 3), (1, 5), (1, 7)):
            source = ag_source(way, hops)

            @pl.when(source // 8 == core)
            def _():
                ag_copy(half, source % 8, way, 1).wait_recv()

    def bias_copy(step, pair):
        where, part = quad(step)
        return pltpu.make_async_remote_copy(
            src_ref=bias_out.at[part, pair], dst_ref=bias_in.at[mine, pair], send_sem=b_send.at[step],
            recv_sem=b_recv.at[mine], device_id=where, device_id_type=MESH,
        )

    def bias_all(step):
        where, part = quad(step)
        return pltpu.make_async_remote_copy(
            src_ref=bias_out.at[part], dst_ref=bias_in.at[part], send_sem=b_send.at[step],
            recv_sem=b_recv.at[part], device_id=where, device_id_type=MESH,
        )

    def forward_pair(pair):
        x_load(pair).wait()
        mats = []
        for r in range(2):
            values = x_v[pair * 2 + r].astype(F32)
            mean = jnp.sum(values, axis=0, keepdims=True) * (1.0 / 64.0)
            centre = values - mean
            inv_std = lax.rsqrt(jnp.sum(centre * centre, axis=0, keepdims=True) * (1.0 / 64.0) + 1e-05)
            stat_v[pair * 2 + r, 0:1, :] = mean
            stat_v[pair * 2 + r, 1:2, :] = inv_std
            mats.append((centre * inv_std * gain_col).astype(BF16))
        pre = dot(w1_v[...], jnp.concatenate(mats, axis=0))
        mixes = []
        for r in range(2):
            gelu_val, gelu_slope = gelu_parts(pre[r * 256:(r + 1) * 256] + bin_col)
            slope_v[pair * 2 + r] = gelu_slope.astype(BF16)
            hidden = gelu_val.astype(BF16)
            onehot = ones_where(bucket_v[pl.ds(pair * 2 + r, 1), :] == iota((32, 1024), 0))
            mixes.append(dot(wmix_v[...], hidden) + dot(tab_v[...], onehot))
        for part in range(4):
            rows = [mix[part * 8:(part + 1) * 8] for mix in mixes]
            bias_out[part, pair] = jnp.concatenate(rows, axis=0).astype(BF16)

    def bias_send(pair):
        for step in (1, 2, 3):
            bias_copy(step, pair).start()

    pl.semaphore_wait(barrier, 14)

    @pl.when(is_home)
    def _():
        k_load.wait()
        v_load.wait()
        for half in range(2):
            for hops in (2, 1):
                ag_copy(half, slot, 0, hops).start()
                ag_copy(half, slot, 1, hops).start()

    for where in (along(2), along(-2), along_x(1), along_x(-1)):
        pl.semaphore_signal(round_one, inc=1, device_id=where, device_id_type=MESH)

    def q_start(at, carry):
        @pl.when(jnp.logical_not(jnp.logical_and(is_home, at == zpos)))
        def _():
            q_copy(at).start()

        return carry

    def forward_body(pair, carry):
        forward_pair(pair)
        bias_send(pair)

        @pl.when(pair == 2)
        def _():
            pl.semaphore_wait(round_one, 4)
            for where in (along(4), along(-4), across_y):
                pl.semaphore_signal(round_two, inc=1, device_id=where, device_id_type=MESH)
            ag_forward(0, 2)

        @pl.when(pair == 3)
        def _():
            ag_forward(1, 2)

        @pl.when(pair == 5)
        def _():
            ag_forward(0, 4)
            pl.semaphore_wait(round_two, 3)
            lax.fori_loop(0, 16, q_start, 0)

        @pl.when(pair == 6)
        def _():
            ag_forward(1, 4)

        return carry

    lax.fori_loop(0, 8, forward_body, 0)

    @pl.when(is_home)
    def _():
        qrecv[slot * 2 + core] = qstage[zpos]

    ag_forward(0, 6)

    def q_wait(at, carry):
        @pl.when(jnp.logical_not(jnp.logical_and(at % 2 == core, core * 8 + at // 2 == zpos)))
        def _():
            q_arrival(at).wait_recv()

        return carry

    lax.fori_loop(0, 16, q_wait, 0)
    arrived = qrecv[...].reshape(512, 128)
    row_a, row_b = iota((512, 512), 0), iota((512, 512), 1)
    order = ones_where(jnp.logical_and(row_a // 8 == row_b % 64, row_a % 8 == row_b // 64))
    by_row = dot(order, arrived).astype(BF16)
    lane, spot = iota((128, 256), 0), iota((128, 256), 1)
    own_head = iota((512, 256), 0) % 8 == iota((512, 256), 1) // 32
    qblk_v[...] = jnp.where(own_head, dot(by_row, ones_where(lane == spot % 32)), 0.0).astype(BF16)
    doblk_v[...] = jnp.where(own_head, dot(by_row, ones_where(lane == 32 + spot % 32)), 0.0).astype(BF16)
    qt_v[...] = qblk_v[...].T
    dot_v[...] = doblk_v[...].T
    wide = iota((128, 128), 0)
    norm_b[...] = dot(by_row, ones_where(jnp.logical_and(wide >= 64, wide < 67)))
    delta_b[...] = dot(by_row, ones_where(jnp.logical_and(wide >= 67, wide < 70)))

    ag_forward(1, 6)
    live = mask_v[...] == 1
    ag_finish(0)
    keys = kv_v[0].reshape(256, 1024)

    for step in (1, 2, 3, 0):
        _, part = quad(step)
        if step:
            bias_all(step).wait_recv()
            bias = bias_in[part]
        else:
            bias = bias_out[part]
        rows = pl.ds(pl.multiple_of(part * 128, 128), 128)
        scores = dot(qblk_v[rows, :], keys) * score_scale + bias.reshape(128, 1024).astype(F32)
        shift = jnp.concatenate([norm_b[rows, :]] * 8, axis=1)
        probs = jnp.where(live, jnp.exp(scores - shift), 0.0)
        probs_f[rows, :] = probs
        probs_v[rows, :] = probs.astype(BF16)
    dkv_v[:, 32:64, :] = dot(dot_v[...], probs_v[...]).reshape(8, 32, 1024)

    def rs_copy(way, far, half):
        hops = 2 if far == 8 or far % 2 == 0 else 1
        send, recv, s_sem, r_sem = (
            (rsp_send, rsp_recv, rp_send, rp_recv), (rsm_send, rsm_recv, rm_send, rm_recv)
        )[way]
        return pltpu.make_async_remote_copy(
            src_ref=send.at[far - 1, half], dst_ref=recv.at[far - 1, half], send_sem=s_sem.at[far - 1, half],
            recv_sem=r_sem.at[far - 1, half], device_id=along(-hops if way else hops), device_id_type=MESH,
        )

    def rs_dest(way, far):
        return (zpos + 16 - far if way else zpos + far) % 16

    def rs_part(far, half, way):
        dest = rs_dest(way, far)
        send, recv = ((rsp_send, rsp_recv), (rsm_send, rsm_recv))[way]
        needed = dest // 8 == core
        if far == 8:
            needed = jnp.logical_and(needed, dest % 2 == way)

        @pl.when(needed)
        def _():
            total = dkv_v[dest % 8, half * 32:half * 32 + 32, :]
            if far in (2, 4, 6):
                for other in (far + 1, far + 2):
                    if other < 8:
                        rs_copy(way, other, half).wait_recv()
                        total = total + recv[other - 1, half].astype(F32)
            send[far - 1, half] = total.astype(BF16)
            if far == 6:
                @pl.when(dest % 2 == way)
                def _():
                    rs_copy(way, 8, half).wait_recv()
                    send[far - 1, half] = (total + recv[7, half].astype(F32)).astype(BF16)

            rs_copy(way, far, half).start()

    def rs_raw(half):
        for far in (8, 7):
            for way in range(2):
                rs_part(far, half, way)

    def rs_sum(far, half):
        for at in (far, far - 1):
            for way in range(2):
                rs_part(at, half, way)

    rs_raw(1)
    ag_finish(1)
    values = kv_v[1].reshape(256, 1024)

    def ds_copy(step, piece):
        where, part = quad(step)
        at = pl.ds(piece * 32, 32)
        return pltpu.make_async_remote_copy(
            src_ref=ds_all.at[part, at], dst_ref=ds_in.at[mine, at], send_sem=d_send.at[step, piece],
            recv_sem=d_recv.at[mine, piece], device_id=where, device_id_type=MESH,
        )

    def ds_arrival(step, piece):
        where, part = quad(step)
        at = pl.ds(pl.multiple_of(piece * 32, 32), 32)
        return pltpu.make_async_remote_copy(
            src_ref=ds_all.at[part, at], dst_ref=ds_in.at[part, at], send_sem=d_send.at[step, piece],
            recv_sem=d_recv.at[part, piece], device_id=where, device_id_type=MESH,
        )

    for step in (1, 3, 2, 0):
        _, part = quad(step)
        rows = pl.ds(pl.multiple_of(part * 128, 128), 128)
        less = jnp.concatenate([delta_b[rows, :]] * 8, axis=1)
        dscores = (probs_f[rows, :] * (dot(doblk_v[rows, :], values) - less)).astype(BF16)
        ds_all[part] = dscores
        if not step:
            ds_in[part] = dscores
    ds_flat = ds_all[...].reshape(512, 1024)
    dkv_v[:, 0:32, :] = dot(qt_v[...], ds_flat).reshape(8, 32, 1024)
    rs_raw(0)
    for step in (1, 3, 2):
        ds_copy(step, 0).start()

    dq_full = lax.dot_general(ds_flat, keys, (((1,), (1,)), ((), ())), preferred_element_type=F32)
    dq_full = jnp.where(own_head, dq_full, 0.0)
    dq_fold = dq_full[:, 0:128] + dq_full[:, 128:256]
    dq_fold = dq_fold + pltpu.roll(dq_fold, 64, 1)
    dq_fold = dq_fold + pltpu.roll(dq_fold, 32, 1)
    group = iota((512, 128), 1) // 32
    h0, h1, h2 = pieces(dq_fold)
    dq_split = jnp.where(group == 0, h0, jnp.where(group == 1, h1, jnp.where(group == 2, h2, 0.0))).astype(BF16)
    back = ones_where(jnp.logical_and(row_b // 8 == row_a % 64, row_b % 8 == row_a // 64))
    dq_head = dot(back, dq_split)
    dq_head = dq_head + pltpu.roll(dq_head, 64, 1)
    dq_head = dq_head + pltpu.roll(dq_head, 32, 1)
    dq_head = dq_head.reshape(16, 32, 128)
    group8 = iota((16, 8, 128), 2) // 32
    dense = dq_head[:, 0:8, :]
    for at in range(1, 4):
        dense = jnp.where(group8 == at, dq_head[:, at * 8:(at + 1) * 8, :], dense)
    dq_send[...] = dense

    def p1_copy(at):
        return pltpu.make_async_remote_copy(
            src_ref=dq_send.at[at], dst_ref=dq_recv.at[zpos], send_sem=p1_send.at[at],
            recv_sem=p1_recv.at[zpos], device_id=device(at % 2, core * 8 + at // 2, ypos), device_id_type=MESH,
        )

    def p1_arrival(at):
        return pltpu.make_async_remote_copy(
            src_ref=dq_send.at[0], dst_ref=dq_recv.at[at], send_sem=p1_send.at[0],
            recv_sem=p1_recv.at[at], device_id=device(home, at, ypos), device_id_type=MESH,
        )

    def p1_start(at, carry):
        @pl.when(jnp.logical_not(jnp.logical_and(at % 2 == core, core * 8 + at // 2 == zpos)))
        def _():
            p1_copy(at).start()

        return carry

    lax.fori_loop(0, 16, p1_start, 0)

    @pl.when(is_home)
    def _():
        dq_recv[zpos] = dq_send[slot * 2 + core]

    rs_sum(6, 1)
    for step in (1, 3, 2):
        ds_copy(step, 1).start()

    def p2_copy(step):
        return pltpu.make_async_remote_copy(
            src_ref=dq_peers.at[key], dst_ref=dq_peers.at[key], send_sem=p2_send.at[step],
            recv_sem=p2_recv.at[key], device_id=(core, (key + step) % 8, col), device_id_type=MESH,
        )

    def p2_arrival(step):
        peer = (key + step) % 8
        return pltpu.make_async_remote_copy(
            src_ref=dq_peers.at[key], dst_ref=dq_peers.at[peer], send_sem=p2_send.at[step],
            recv_sem=p2_recv.at[peer], device_id=(core, peer, col), device_id_type=MESH,
        )

    def phase_two():
        def p1_wait(at, carry):
            @pl.when(jnp.logical_not(jnp.logical_and(is_home, at == zpos)))
            def _():
                p1_arrival(at).wait_recv()

            return carry

        lax.fori_loop(0, 16, p1_wait, 0)
        dq_peers[key] = dq_recv[...].reshape(128, 128).astype(BF16)

        def p2_start(step, carry):
            p2_copy(step).start()
            return carry

        lax.fori_loop(1, 8, p2_start, 0)

    win = win_v[...]

    def gp_copy(pair):
        return pltpu.make_async_copy(gp_v.at[pl.ds(pair * 2, 2)], gp_hbm.at[pl.ds(pair * 2, 2)], gp_sem.at[pair])

    def backward_pair(pair):
        at = pl.ds(pl.multiple_of(pair * 16, 16), 16)
        dhidden = dot(w2_v[...], ds_in[:, at, :].reshape(64, 1024))
        for r in range(2):
            row = pair * 2 + r
            dpre = (dhidden[r * 256:(r + 1) * 256] * slope_v[row].astype(F32)).astype(BF16)
            dunit = dot(win, dpre) * gain_col
            inv_std = stat_v[row, 1:2, :]
            unit = (x_v[row].astype(F32) - stat_v[row, 0:1, :]) * inv_std
            first = jnp.sum(dunit, axis=0, keepdims=True) * (1.0 / 64.0)
            second = jnp.sum(dunit * unit, axis=0, keepdims=True) * (1.0 / 64.0)
            gp_v[row] = (inv_std * (dunit - first - unit * second)).astype(BF16)
        gp_copy(pair).start()

    def backward_body(pair, carry):
        @pl.when(pair % 2 == 0)
        def _():
            for step in (1, 2, 3):
                ds_arrival(step, pair // 2).wait_recv()

        backward_pair(pair)
        for at in (0, 2):
            @pl.when(pair == at)
            def _():
                for step in (1, 3, 2):
                    ds_copy(step, at // 2 + 2).start()

        for at, (far, half) in ((0, (6, 0)), (1, (4, 1)), (3, (4, 0)), (4, (2, 1))):
            @pl.when(pair == at)
            def _():
                rs_sum(far, half)

        @pl.when(pair == 6)
        def _():
            phase_two()

        return carry

    lax.fori_loop(0, 8, backward_body, 0)
    rs_sum(2, 0)

    sibling, _ = quad(2)

    def f_copy():
        return pltpu.make_async_remote_copy(
            src_ref=gkv_v, dst_ref=gkv_v, send_sem=f_send, recv_sem=f_recv,
            device_id=sibling, device_id_type=MESH,
        )

    @pl.when(is_home)
    def _():
        total = dkv_v[slot]
        for way, recv in ((0, rsp_recv), (1, rsm_recv)):
            for far in (1, 2):
                for half in range(2):
                    rs_copy(way, far, half).wait_recv()
                total = total + recv[far - 1].reshape(64, 1024).astype(F32)
        gkv_v[0:32, :] = (total[0:32] * score_scale).astype(BF16)
        gkv_v[32:64, :] = total[32:64].astype(BF16)
        f_copy().start()

    def p2_wait(step, carry):
        p2_arrival(step).wait_recv()
        return carry

    lax.fori_loop(1, 8, p2_wait, 0)
    total_q = dq_peers[0].astype(F32)
    for at in range(1, 8):
        total_q = total_q + dq_peers[at].astype(F32)
    final_q = (total_q * score_scale).astype(BF16).astype(F32).T.astype(BF16)
    lane_a, lane_b = iota((128, 512), 0), iota((128, 512), 1)
    grad_q = jnp.zeros((32, 512), F32)
    for at in range(4):
        place = jnp.logical_and(
            lane_a // 8 == lane_b // 32,
            jnp.logical_and(lane_a % 8 == lane_b % 8, (lane_b // 8) % 4 == at),
        )
        grad_q = grad_q + dot(final_q[at * 32:(at + 1) * 32, :], ones_where(place))
    gq_v[...] = grad_q.astype(BF16)
    gq_copy = pltpu.make_async_copy(gq_v, gq_hbm.at[0], o_sem.at[0])
    gq_copy.start()

    @pl.when(jnp.logical_not(is_home))
    def _():
        f_copy().wait_recv()

    gk_copy = pltpu.make_async_copy(gkv_v.at[pl.ds(0, 32)], gk_hbm.at[0], o_sem.at[1])
    gv_copy = pltpu.make_async_copy(gkv_v.at[pl.ds(32, 32)], gv_hbm.at[0], o_sem.at[2])
    gk_copy.start()
    gv_copy.start()

    @pl.when(is_home)
    def _():
        f_copy().wait_send()
        for half in range(2):
            for hops in (2, 1):
                ag_copy(half, slot, 0, hops).wait_send()
                ag_copy(half, slot, 1, hops).wait_send()

    for half in range(2):
        for hops in (2, 4, 6):
            ag_forward(half, hops, True)

    def z_drain(at, carry):
        @pl.when(jnp.logical_not(jnp.logical_and(is_home, at == zpos)))
        def _():
            q_copy(at).wait_send()

        @pl.when(jnp.logical_not(jnp.logical_and(at % 2 == core, core * 8 + at // 2 == zpos)))
        def _():
            p1_copy(at).wait_send()

        return carry

    lax.fori_loop(0, 16, z_drain, 0)
    for step in (1, 2, 3):
        bias_all(step).wait_send()
        for piece in range(4):
            ds_copy(step, piece).wait_send()

    for half in range(2):
        for way in range(2):
            for far in range(1, 9):
                dest = rs_dest(way, far)
                sent = dest // 8 == core
                if far == 8:
                    sent = jnp.logical_and(sent, dest % 2 == way)

                @pl.when(sent)
                def _():
                    rs_copy(way, far, half).wait_send()

    def last_drain(step, carry):
        p2_copy(step).wait_send()
        return carry

    lax.fori_loop(1, 8, last_drain, 0)

    def gp_drain(pair, carry):
        gp_copy(pair).wait()
        return carry

    lax.fori_loop(0, 8, gp_drain, 0)
    gq_copy.wait()
    gk_copy.wait()
    gv_copy.wait()


def hand_over(gp_in, gq_in, gk_in, gv_in, gp_out, gq_out, gk_out, gv_out, gp_v, gq_v, gk_v, gv_v, in_sem, out_sem):
    stages = [(gq_in, gq_v, gq_out), (gk_in, gk_v, gk_out), (gv_in, gv_v, gv_out)]
    for at in range(8):
        rows = pl.ds(at * 2, 2)
        stages.append((gp_in.at[rows], gp_v.at[rows], gp_out.at[rows]))
    loads = [pltpu.make_async_copy(src, mid, in_sem.at[at]) for at, (src, mid, _) in enumerate(stages)]
    stores = [pltpu.make_async_copy(mid, dst, out_sem.at[at]) for at, (_, mid, dst) in enumerate(stages)]
    for load in loads:
        load.start()
    for load, store in zip(loads, stores):
        load.wait()
        store.start()
    for store in stores:
        store.wait()


def per_device(
    pair_feats, bucket_ids, ln_gain, w_in, b_in, w_out, bucket_table, key_mask,
    q_heads, k_heads, v_heads, out_heads, dout_heads, log_norm,
):
    any_space = pl.BlockSpec(memory_space=pl.ANY)
    vmem = pltpu.VMEM
    dma = pltpu.SemaphoreType.DMA
    results = pl.pallas_call(
        kernel,
        out_shape=(
            jax.ShapeDtypeStruct((16, 64, 1024), BF16),
            jax.ShapeDtypeStruct((1, 32, 512), BF16),
            jax.ShapeDtypeStruct((1, 32, 1024), BF16),
            jax.ShapeDtypeStruct((1, 32, 1024), BF16),
        ),
        in_specs=[any_space] * 14,
        out_specs=(any_space,) * 4,
        scratch_shapes=[
            vmem((16, 64, 1024), BF16),
            vmem((16, 1024), jnp.int32),
            vmem((1, 64), F32),
            vmem((64, 256), BF16),
            vmem((1, 256), F32),
            vmem((32, 256), BF16),
            vmem((32, 32), BF16),
            vmem((1, 1024), jnp.int32),
            vmem((1, 32, 512), BF16),
            vmem((1, 32, 512), BF16),
            vmem((1, 32, 512), BF16),
            vmem((1, 512), F32),
            vmem((16, 64, 1024), BF16),
            vmem((32, 512), BF16),
            vmem((64, 1024), BF16),
            vmem((16, 256, 1024), BF16),
            vmem((16, 2, 1024), F32),
            vmem((2, 8, 32, 1024), BF16),
            vmem((4, 8, 16, 1024), BF16),
            vmem((4, 8, 16, 1024), BF16),
            vmem((4, 128, 1024), BF16),
            vmem((4, 128, 1024), BF16),
            vmem((512, 1024), BF16),
            vmem((512, 1024), F32),
            vmem((16, 32, 128), BF16),
            vmem((16, 32, 128), BF16),
            vmem((512, 256), BF16),
            vmem((512, 256), BF16),
            vmem((256, 512), BF16),
            vmem((256, 512), BF16),
            vmem((512, 128), F32),
            vmem((512, 128), F32),
            vmem((8, 64, 1024), F32),
            vmem((8, 2, 32, 1024), BF16),
            vmem((8, 2, 32, 1024), BF16),
            vmem((8, 2, 32, 1024), BF16),
            vmem((8, 2, 32, 1024), BF16),
            vmem((16, 8, 128), F32),
            vmem((16, 8, 128), F32),
            vmem((8, 128, 128), BF16),
            vmem((512, 128), BF16),
            vmem((512, 64), BF16),
            vmem((32, 256), BF16),
            vmem((32, 32), BF16),
            dma((11,)), dma((8,)), dma((2,)), dma((8,)), dma((3,)),
            dma((2, 4, 8)), dma((2, 8)), dma((16,)), dma((16,)), dma((4,)), dma((4,)), dma((4, 4)), dma((4, 4)),
            dma((8, 2)), dma((8, 2)), dma((8, 2)), dma((8, 2)), dma, dma,
            dma((16,)), dma((16,)), dma((8,)), dma((8,)),
            pltpu.SemaphoreType.REGULAR, pltpu.SemaphoreType.REGULAR,
        ],
        compiler_params=pltpu.CompilerParams(
            collective_id=0, has_side_effects=True, vmem_limit_bytes=56 * 2**20
        ),
        name="pair_attention_backward",
    )(
        pair_feats, bucket_ids, ln_gain.reshape(1, 64), w_in, b_in.reshape(1, 256), w_out.T,
        bucket_table, key_mask.reshape(1, 1024), q_heads, k_heads, v_heads, out_heads, dout_heads, log_norm,
    )
    return pl.pallas_call(
        hand_over,
        out_shape=tuple(jax.ShapeDtypeStruct(member.shape, member.dtype) for member in results),
        in_specs=[any_space] * 4,
        out_specs=(any_space,) * 4,
        scratch_shapes=[
            vmem((16, 64, 1024), BF16), vmem((1, 32, 512), BF16), vmem((1, 32, 1024), BF16), vmem((1, 32, 1024), BF16),
            dma((11,)), dma((11,)),
        ],
        name="hand_over",
    )(*results)


def solution(mesh):
    return jax.shard_map(
        per_device,
        mesh=mesh,
        in_specs=(
            P(("query", "heads"), None, "key"),
            P(("query", "heads"), "key"),
            P(),
            P(),
            P(),
            P(),
            P(),
            P("key"),
            P("heads", None, "query"),
            P("heads", None, "key"),
            P("heads", None, "key"),
            P("heads", None, "query"),
            P("heads", None, "query"),
            P("heads", "query"),
        ),
        out_specs=(
            P(("query", "heads"), None, "key"),
            P("heads", None, "query"),
            P("heads", None, "key"),
            P("heads", None, "key"),
        ),
        check_vma=False,
    )
```
